32 devices in a mesh: gz: 4 (over z), gy: 8 (over y, x, core).
Axes of the slice: x: 2, y: 2, z: 4, core: 2. Of those that a mesh axis runs over, the one named last changes fastest.
Arguments:
- thermal_departure: float32 [8, 1024, 1024], P(None, 'gy', 'gz'), may hold values from -6 to 6
- speed_along_primary: float32 [8, 1024, 1024], P(None, 'gy', 'gz'), may hold values from -4 to 4
- speed_along_lateral: float32 [8, 1024, 1024], P(None, 'gy', 'gz'), may hold values from -4 to 4
- upward_speed: float32 [8, 1024, 1024], P(None, 'gy', 'gz'), may hold values from -4 to 4
- container_solid_markers: int32 [8, 1024, 1024], P(None, 'gy', 'gz'), may hold values 0 or 1
Outputs:
- temp_next: float32 [8, 1024, 1024], P(None, 'gy', 'gz')
- u_next: float32 [8, 1024, 1024], P(None, 'gy', 'gz')
- v_next: float32 [8, 1024, 1024], P(None, 'gy', 'gz')
- w_next: float32 [8, 1024, 1024], P(None, 'gy', 'gz')
- path_map: float32 [8, 1024], P('gz', 'gy')
The draws below stay inside these ranges and needn't reach their ends.
Inputs may be any that keep to these rules, and one draw needn't show every extreme that they name: `container_solid_markers`: 1 marks air, 0 a solid cell.
All inputs are finite; a program needn't handle non-finite values. No bound on the sum of `container_solid_markers` on one device may be relied on, other than what follows from the above.
Results may differ from the reference program's by a relative error of at most 0.00002.
Values sent between devices are 32-bit elements; how exact they have to be, the bound alone decides.
No kernel may reach another device: no remote copies, remote signals or barrier semaphores. Data moves between devices by JAX's collectives and lax.ppermute only.
A program may use at most 128 MiB of HBM per device.

```python
import math
import jax
import jax.numpy as jnp
from jax import lax

SHEET_ROW_COUNT = 8
CY = 128
LATERAL_COUNT = 1024
ALTITUDE_COUNT = 1024
N_GY = 8


def with_ends(entries, own_key, low, high):
    extent = entries.shape
    place = [jax.random.randint(jax.random.fold_in(own_key, axis), (), 0, extent[axis]) for axis in range(len(extent))]
    entries = entries.at[tuple(place)].set(low)
    longest = extent.index(max(extent))
    place[longest] = (place[longest] + 1) % extent[longest]
    return entries.at[tuple(place)].set(high)


def shard_levels(key, dims, shards, smallest, top_value):
    factor_of, own = 1.0, jax.random.fold_in(key, 6)
    for dim, parts in shards:
        draws = jnp.exp(jax.random.uniform(jax.random.fold_in(own, dim), (parts,), jnp.float32, smallest / len(shards), top_value / len(shards)))
        factor_of = factor_of * jnp.repeat(draws, dims[dim] // parts).reshape([-1 if axis == dim else 1 for axis in range(len(dims))])
    return factor_of


def gaussian(stream_key, dims, spread, bound, split=(), held_as=jnp.bfloat16):
    result = jax.random.normal(stream_key, dims, jnp.float32) * spread
    if len(split) > 0:
        result = shard_levels(stream_key, dims, split, -0.22, 0.18) * result
    return jnp.clip(result, min=-bound, max=bound).astype(held_as)


def setup_inputs(seed: int = 0) -> dict:
    key_of = jax.random.split(jax.random.key(seed), 6)
    thermal_departure = gaussian(key_of[0], (SHEET_ROW_COUNT, LATERAL_COUNT, ALTITUDE_COUNT), 1.0, 6.0, ((1, 8), (2, 4)), jnp.float32)
    speed_along_primary = gaussian(key_of[1], (SHEET_ROW_COUNT, LATERAL_COUNT, ALTITUDE_COUNT), 1.0, 4.0, ((1, 8), (2, 4)), jnp.float32)
    speed_along_lateral = gaussian(key_of[2], (SHEET_ROW_COUNT, LATERAL_COUNT, ALTITUDE_COUNT), 1.0, 4.0, ((1, 8), (2, 4)), jnp.float32)
    upward_speed = gaussian(key_of[3], (SHEET_ROW_COUNT, LATERAL_COUNT, ALTITUDE_COUNT), 1.0, 4.0, ((1, 8), (2, 4)), jnp.float32)
    container_solid_markers = with_ends((jax.random.randint(key_of[4], (SHEET_ROW_COUNT, LATERAL_COUNT, ALTITUDE_COUNT), 0, 8) < 7).astype(jnp.int32), jax.random.fold_in(key_of[4], 1), 0, 1)
    return dict(thermal_departure=thermal_departure, speed_along_primary=speed_along_primary, speed_along_lateral=speed_along_lateral, upward_speed=upward_speed, container_solid_markers=container_solid_markers)


TIME_STEP = 0.1
NU_BASE = 0.05
KAPPA_BASE = 0.05
SMAG_COEF = 0.03
PRANDTL = 0.4
BUOYANCY = 0.5

def tendencies(padded):
    centre = padded[:, :, 1:-1, 1:-1]
    east_side = jnp.roll(centre, -1, 1)
    west_side = jnp.roll(centre, 1, 1)
    north_side = padded[:, :, 2:, 1:-1]
    south_side = padded[:, :, :-2, 1:-1]
    upper_side = padded[:, :, 1:-1, 2:]
    lower_side = padded[:, :, 1:-1, :-2]
    grad_x = 0.5 * (east_side - west_side)
    grad_y = 0.5 * (north_side - south_side)
    grad_z = 0.5 * (upper_side - lower_side)
    laplace = east_side + west_side + north_side + south_side + upper_side + lower_side - 6.0 * centre
    advect = centre[1] * grad_x + centre[2] * grad_y + centre[3] * grad_z
    strain = grad_x[1] * grad_x[1] + grad_y[2] * grad_y[2] + grad_z[3] * grad_z[3]
    shear_a = grad_y[1] + grad_x[2]
    shear_b = grad_z[1] + grad_x[3]
    shear_c = grad_z[2] + grad_y[3]
    strain = strain + 0.5 * (shear_a * shear_a + shear_b * shear_b + shear_c * shear_c)
    eddy_visc = SMAG_COEF * jnp.sqrt(2.0 * strain + 0.01)
    diffusion = jnp.stack([KAPPA_BASE + eddy_visc / PRANDTL, NU_BASE + eddy_visc, NU_BASE + eddy_visc, NU_BASE + eddy_visc])
    tendency = diffusion * laplace - advect
    buoyant = tendency[3] + BUOYANCY * centre[0]
    return jnp.stack([tendency[0], tendency[1], tendency[2], buoyant])

def masked(fluid_unknowns, fluid_mask):
    return jnp.concatenate([fluid_unknowns[:1], fluid_unknowns[1:] * fluid_mask[None]], 0)

def full_rates(fluid_unknowns):
    wrapped = jnp.concatenate([fluid_unknowns[:, :, -1:], fluid_unknowns, fluid_unknowns[:, :, :1]], 2)
    padded = jnp.pad(wrapped, ((0, 0), (0, 0), (0, 0), (1, 1)))

    def by_block(block_index):
        piece = lax.dynamic_slice_in_dim(padded, block_index * CY, CY + 2, 2)
        return tendencies(piece)
    pieces = lax.map(by_block, jnp.arange(N_GY, dtype=jnp.int32))
    return jnp.moveaxis(pieces, 0, 2).reshape(4, SHEET_ROW_COUNT, LATERAL_COUNT, ALTITUDE_COUNT)

def reference(thermal_departure, speed_along_primary, speed_along_lateral, upward_speed, container_solid_markers):
    fluid_mask = container_solid_markers.astype(jnp.float32)
    fluid_unknowns = jnp.stack([thermal_departure, speed_along_primary, speed_along_lateral, upward_speed])
    section_one = masked(fluid_unknowns + TIME_STEP * full_rates(fluid_unknowns), fluid_mask)
    section_two = masked(0.5 * fluid_unknowns + 0.5 * (section_one + TIME_STEP * full_rates(section_one)), fluid_mask)
    refraction = 8.0 * (1.0 - jnp.exp(-section_two[0] / 8.0))
    path_map = lax.optimization_barrier(jnp.sum(refraction, axis=2)) / math.sqrt(ALTITUDE_COUNT)
    return (section_two[0], section_two[1], section_two[2], section_two[3], path_map)
```

```python
import functools
import math

import jax
import jax.numpy as jnp
from jax import lax
from jax.experimental import pallas as pl
from jax.experimental.pallas import tpu as pltpu
from jax.sharding import PartitionSpec as P

TIME_STEP = 0.1
NU_BASE = 0.05
KAPPA_BASE = 0.05
SMAG_COEF = 0.03
PRANDTL = 0.4
BUOYANCY = 0.5
LANES = 128
PAD = 8
LIMIT = 16 << 20
HBM = pl.BlockSpec(memory_space=pltpu.HBM)
VMEM = pl.BlockSpec(memory_space=pltpu.VMEM)


def lane_iota():
    return lax.broadcasted_iota(jnp.int32, (8, LANES), 1)


def stepped(base, c, e, w, n, s, u, l, scale):
    h = TIME_STEP * scale
    dx = [a - b for a, b in zip(e, w)]
    dy = [a - b for a, b in zip(n, s)]
    dz = [a - b for a, b in zip(u, l)]
    lap = [
        ((a + b) + (p + q)) + ((r + t) - 6.0 * m)
        for a, b, p, q, r, t, m in zip(e, w, n, s, u, l, c)
    ]
    straight = dx[1] * dx[1] + dy[2] * dy[2] + dz[3] * dz[3]
    shear_a = dy[1] + dx[2]
    shear_b = dz[1] + dx[3]
    shear_c = dz[2] + dy[3]
    shear = shear_a * shear_a + shear_b * shear_b + shear_c * shear_c
    k = (SMAG_COEF * h) ** 2
    arg = (straight + straight + shear) * (0.25 * k) + 0.01 * k
    eddy = arg * lax.rsqrt(arg)
    c_mom = eddy + NU_BASE * h
    c_heat = eddy * (1.0 / PRANDTL) + KAPPA_BASE * h
    vel = [(0.5 * h) * q for q in c[1:]]
    out = []
    for i in range(4):
        coef = c_heat if i == 0 else c_mom
        adv = vel[0] * dx[i] + vel[1] * dy[i] + vel[2] * dz[i]
        out.append((base[i] + coef * lap[i]) - adv)
    out[3] = out[3] + (BUOYANCY * h) * c[0]
    return out


def lane_next(blocks, lane):
    r = [pltpu.roll(b, LANES - 1, 1) for b in blocks]
    if len(r) == 1:
        return r
    return [jnp.where(lane == LANES - 1, r[(i + 1) % len(r)], r[i]) for i in range(len(r))]


def lane_prev(blocks, lane):
    r = [pltpu.roll(b, 1, 1) for b in blocks]
    if len(r) == 1:
        return r
    return [jnp.where(lane == 0, r[i - 1], r[i]) for i in range(len(r))]


def height_pair(blocks, lane):
    count = len(blocks)
    up = [pltpu.roll(b, LANES - 1, 1) for b in blocks]
    lo = [pltpu.roll(b, 1, 1) for b in blocks]
    upper = [
        up[i] if i == count - 1 else jnp.where(lane == LANES - 1, up[i + 1], up[i])
        for i in range(count)
    ]
    lower = [lo[i] if i == 0 else jnp.where(lane == 0, lo[i - 1], lo[i]) for i in range(count)]
    return upper, lower


def east(q):
    return pltpu.roll(q, 7, 0)


def west(q):
    return pltpu.roll(q, 1, 0)


def flat(ref):
    return ref.reshape(math.prod(ref.shape[:-1]), LANES)


def row_of(ref, lead, x_stride, start, x):
    return ref[pl.ds(lead + start, x, stride=x_stride), :]


def pack_kernel(dims, *refs):
    x_n, h_n, ny = dims
    ins = refs[:5]
    s0, mk, ys_a, ys_b, zown, part, turned, sem = refs[5:]
    nyp = ny + 2 * PAD
    lane = lane_iota()
    copies = []
    for f in range(5):
        for h in range(h_n):
            dst = s0.at[f] if f < 4 else mk
            copies.append(
                pltpu.make_async_copy(
                    ins[f].at[:, :, pl.ds(h * LANES, LANES)],
                    dst.at[:, h, pl.ds(PAD, ny), :],
                    sem.at[f, h],
                )
            )
    for c in copies:
        c.start()
    for c in copies:
        c.wait()
    even = lax.rem(lax.axis_index("gy"), 2) == 0
    s0_flat, mk_flat = flat(s0), flat(mk)
    stride = h_n * nyp

    def rows(dst, ys):
        for r, y in enumerate(ys):
            for h in range(h_n):
                cols = slice(h * LANES, (h + 1) * LANES)
                for f in range(4):
                    block = row_of(s0_flat, (f * x_n * h_n + h) * nyp, stride, PAD + y, x_n)
                    dst[(r * 4 + f) * 8 : (r * 4 + f) * 8 + 8, cols] = block
                if r == 0:
                    block = row_of(mk_flat, h * nyp, stride, PAD + y, x_n)
                    dst[64:72, cols] = block.astype(jnp.float32)

    first, last = (0, 1), (ny - 1, ny - 2)

    @pl.when(even)
    def _():
        rows(ys_a, last)
        rows(ys_b, first)

    @pl.when(jnp.logical_not(even))
    def _():
        rows(ys_a, first)
        rows(ys_b, last)

    group = lane // 8

    def tile(t, carry):
        y = pl.multiple_of(PAD + t * 8, 8)
        yo = pl.multiple_of(t * 8, 8)
        for a in range(3):
            acc = jnp.zeros((8, LANES), jnp.float32)
            for g in range(16 if a < 2 else 8):
                f, x = a * 2 + g // 8, g % 8
                if a < 2:
                    lo, hi = s0[f, x, 0, pl.ds(y, 8), :], s0[f, x, h_n - 1, pl.ds(y, 8), :]
                else:
                    lo, hi = mk[x, 0, pl.ds(y, 8), :], mk[x, h_n - 1, pl.ds(y, 8), :]
                both = jnp.where(lane < LANES // 2, lo, hi).astype(jnp.float32)
                acc = jnp.where(group == g, pltpu.roll(both, (g * 8 + 4) % LANES, 1), acc)
            part[a, pl.ds(yo, 8), :] = acc
        return carry

    lax.fori_loop(0, ny // 8, tile, 0, unroll=2)
    for a in range(3):
        for b in range(ny // LANES):
            cols = slice(b * LANES, (b + 1) * LANES)
            turned[a, b] = part[a, cols, :].T
    for side in range(2):
        for l in range(4):
            j = 4 + l if side == 0 else 3 - l
            for b in range(ny // LANES):
                cols = slice(b * LANES, (b + 1) * LANES)
                for f in range(4):
                    k = f * 4 + l
                    zown[side, k * 8 : k * 8 + 8, cols] = turned[
                        f // 2, b, pl.ds((f % 2) * 64 + j, 8, stride=8), :
                    ]
                if l < 3:
                    k = 16 + l
                    zown[side, k * 8 : k * 8 + 8, cols] = turned[2, b, pl.ds(j, 8, stride=8), :]


def y_halo(even, a_ref, b_ref, k, cols):
    a, b = a_ref[k * 8 : k * 8 + 8, cols], b_ref[k * 8 : k * 8 + 8, cols]
    return jnp.where(even, b, a), jnp.where(even, a, b)


def beyond(lane, even, ya, yb, h_n, side, f, l, rows):
    h = 0 if side == 0 else h_n - 1
    at = l if side == 0 else LANES - 1 - l
    out = jnp.zeros((8, LANES), jnp.float32)
    for r in rows:
        k = r * 4 + f if f < 4 else 8
        before, after = y_halo(even, ya, yb, k, slice(h * LANES, (h + 1) * LANES))
        out = jnp.where(
            lane == LANES - 1 - r, pltpu.roll(before, (LANES - 1 - r - at) % LANES, 1), out
        )
        out = jnp.where(lane == r, pltpu.roll(after, (r - at) % LANES, 1), out)
    return out


def corner_kernel(dims, ya, yb, zown, zs_a, zs_b):
    x_n, h_n, ny = dims
    lane = lane_iota()
    even = lax.rem(lax.axis_index("gy"), 2) == 0
    even_z = lax.rem(lax.axis_index("gz"), 2) == 0

    def strip(dst, side):
        for l in range(2):
            for f in range(4):
                k, m = l * 4 + f, f * 4 + l
                dst[k * 8 : k * 8 + 8, :] = zown[side, m * 8 : m * 8 + 8, :]
        dst[64:72, :] = zown[side, 128:136, :]
        for f in range(4):
            dst[72 + f * 8 : 80 + f * 8, 0:LANES] = beyond(
                lane, even, ya, yb, h_n, side, f, 0, (0,)
            )
            if ny > LANES:
                dst[72 + f * 8 : 80 + f * 8, LANES:] = jnp.zeros((8, ny - LANES), jnp.float32)

    @pl.when(even_z)
    def _():
        strip(zs_a, 1)
        strip(zs_b, 0)

    @pl.when(jnp.logical_not(even_z))
    def _():
        strip(zs_a, 0)
        strip(zs_b, 1)


def load4(ref, x, h, y):
    return [ref[f, x, h, pl.ds(y, 8), :] for f in range(4)]


def section_one_kernel(dims, s0, mk, s1):
    x_n, h_n, ny = dims
    lane = lane_iota()

    def tile(y, x):
        c = [load4(s0, x, h, y) for h in range(h_n)]
        pairs = [height_pair([c[h][f] for h in range(h_n)], lane) for f in range(4)]
        for h in range(h_n):
            r = stepped(
                c[h],
                c[h],
                load4(s0, (x + 1) % x_n, h, y),
                load4(s0, (x - 1) % x_n, h, y),
                load4(s0, x, h, y + 1),
                load4(s0, x, h, y - 1),
                [p[0][h] for p in pairs],
                [p[1][h] for p in pairs],
                1.0,
            )
            open_cell = mk[x, h, pl.ds(y, 8), :] != 0
            s1[0, x, h, pl.ds(y, 8), :] = r[0]
            for f in range(1, 4):
                s1[f, x, h, pl.ds(y, 8), :] = jnp.where(open_cell, r[f], 0.0)

    def body(t, carry):
        for j in range(2):
            y = pl.multiple_of(PAD + t * 16 + j * 8, 8)
            for x in range(x_n):
                tile(y, x)
        return carry

    lax.fori_loop(0, ny // 16, body, 0)


def section_two_kernel(dims, s0, mk, s1, s2, path, acc):
    x_n, h_n, ny = dims
    lane = lane_iota()

    def tile(y, yo, x):
        c = [load4(s1, x, h, y) for h in range(h_n)]
        pairs = [height_pair([c[h][f] for h in range(h_n)], lane) for f in range(4)]
        total = None
        for h in range(h_n):
            start = load4(s0, x, h, y)
            r = stepped(
                [0.5 * (a + b) for a, b in zip(start, c[h])],
                c[h],
                load4(s1, (x + 1) % x_n, h, y),
                load4(s1, (x - 1) % x_n, h, y),
                load4(s1, x, h, y + 1),
                load4(s1, x, h, y - 1),
                [p[0][h] for p in pairs],
                [p[1][h] for p in pairs],
                0.5,
            )
            open_cell = mk[x, h, pl.ds(y, 8), :] != 0
            cols = slice(h * LANES, (h + 1) * LANES)
            s2[0, x, pl.ds(yo, 8), cols] = r[0]
            for f in range(1, 4):
                s2[f, x, pl.ds(yo, 8), cols] = jnp.where(open_cell, r[f], 0.0)
            refr = 1.0 - jnp.exp(r[0] * (-0.125))
            if h == 0:
                refr = jnp.where(lane < 2, 0.0, refr)
            if h == h_n - 1:
                refr = jnp.where(lane >= LANES - 2, 0.0, refr)
            total = refr if total is None else total + refr
        acc[x, pl.ds(yo, 8), :] = total

    def body(t, carry):
        for j in range(2):
            y = pl.multiple_of(PAD + t * 16 + j * 8, 8)
            yo = pl.multiple_of(t * 16 + j * 8, 8)
            for x in range(x_n):
                tile(y, yo, x)
        return carry

    lax.fori_loop(0, ny // 16, body, 0)
    for x in range(x_n):
        for b in range(ny // LANES):
            cols = slice(b * LANES, (b + 1) * LANES)
            path[x : x + 1, cols] = jnp.sum(acc[x, cols, :].T, axis=0, keepdims=True)


def edge_kernel(dims, count_z, *refs):
    x_n, h_n, ny = dims
    s0, mk, s1, zown, ya, yb, za, zb, path_in = refs[:9]
    zp, yp, own = refs[9:12]
    sends = refs[12 : 12 + count_z - 1]
    turned, path = refs[12 + count_z - 1 :]
    nyp = ny + 2 * PAD
    nb = ny // LANES
    lane = lane_iota()
    even = lax.rem(lax.axis_index("gy"), 2) == 0
    gz = lax.axis_index("gz")
    even_z = lax.rem(gz, 2) == 0
    s0_flat, s1_flat, mk_flat = flat(s0), flat(s1), flat(mk)
    stride = h_n * nyp
    blk = [slice(b * LANES, (b + 1) * LANES) for b in range(max(nb, h_n))]

    y_sums = []
    for side in range(2):

        def at(r):
            return PAD + (r if side == 0 else ny - 1 - r)

        def own_rows(ref, r):
            return [
                [row_of(ref, (f * x_n * h_n + h) * nyp, stride, at(r), x_n) for h in range(h_n)]
                for f in range(4)
            ]

        def halo(k):
            return [y_halo(even, ya, yb, k, blk[h])[side] for h in range(h_n)]

        zero = {
            -2: [halo(4 + f) for f in range(4)],
            -1: [halo(f) for f in range(4)],
        }
        for r in range(3):
            zero[r] = own_rows(s0_flat, r)
        open_at = {-1: [m != 0.0 for m in halo(8)]}
        for r in range(2):
            open_at[r] = [
                row_of(mk_flat, h * nyp, stride, at(r), x_n) != 0 for h in range(h_n)
            ]
        one = {r: own_rows(s1_flat, r) for r in (1, 2)}

        def advance(state, base, r, scale, fields=4):
            pairs = [height_pair(state[r][f], lane) for f in range(4)]
            ahead, behind = (r + 1, r - 1) if side == 0 else (r - 1, r + 1)
            out = [[None] * h_n for _ in range(4)]
            for h in range(h_n):
                c = [state[r][f][h] for f in range(4)]
                q = stepped(
                    [base[f][h] for f in range(4)],
                    c,
                    [east(v) for v in c],
                    [west(v) for v in c],
                    [state[ahead][f][h] for f in range(4)],
                    [state[behind][f][h] for f in range(4)],
                    [p[0][h] for p in pairs],
                    [p[1][h] for p in pairs],
                    scale,
                )
                for f in range(4):
                    out[f][h] = q[f] if f == 0 else jnp.where(open_at[r][h], q[f], 0.0)
            return out

        for r in (-1, 0):
            one[r] = advance(zero, zero[r], r, 1.0)
        for r in (0, 1):
            base = [
                [0.5 * (zero[r][f][h] + one[r][f][h]) for h in range(h_n)] for f in range(4)
            ]
            two = advance(one, base, r, 0.5)
            for f in range(4):
                for h in range(h_n):
                    yp[side * 8 + r * 4 + f, :, blk[h]] = two[f][h]
            total = None
            for h in range(h_n):
                refr = 1.0 - jnp.exp(two[0][h] * (-0.125))
                if h == 0:
                    refr = jnp.where(lane < 2, 0.0, refr)
                if h == h_n - 1:
                    refr = jnp.where(lane >= LANES - 2, 0.0, refr)
                total = refr if total is None else total + refr
            y_sums.append((r if side == 0 else ny - 1 - r, jnp.sum(total, axis=1, keepdims=True)))

    sums = [path_in[:, blk[b]] for b in range(nb)]
    for y, value in y_sums:
        b = y // LANES
        sums[b] = jnp.where(lane == y % LANES, value, sums[b])

    for side in range(2):
        exists = (gz > 0) if side == 0 else (gz < count_z - 1)

        def halo(k):
            cols = [slice(b * LANES, (b + 1) * LANES) for b in range(nb)]
            rows = slice(k * 8, k * 8 + 8)
            take_a = jnp.logical_not(even_z) if side == 0 else even_z
            return [jnp.where(take_a, za[rows, c], zb[rows, c]) for c in cols]

        def mine(k):
            return [zown[side, k * 8 : k * 8 + 8, blk[b]] for b in range(nb)]

        def extra(f, l, rows):
            return [beyond(lane, even, ya, yb, h_n, side, f, l, rows)]

        blank = [jnp.zeros((8, LANES), jnp.float32)]
        zero = {
            -2: [halo(4 + f) + blank for f in range(4)],
            -1: [halo(f) + halo(9 + f)[:1] for f in range(4)],
        }
        for l in range(4):
            zero[l] = [
                mine(f * 4 + l) + (extra(f, l, (0, 1)) if l < 3 else blank) for f in range(4)
            ]
        open_at = {-1: [m != 0.0 for m in halo(8)]}
        for l in range(3):
            open_at[l] = [m != 0.0 for m in mine(16 + l)]
        for l in range(2):
            open_at[l] = open_at[l] + [extra(4, l, (0,))[0] != 0.0]

        def advance(state, base, l, scale, blocks):
            norths = [lane_next(state[l][f], lane) for f in range(4)]
            souths = [lane_prev(state[l][f], lane) for f in range(4)]
            above, below = (l + 1, l - 1) if side == 0 else (l - 1, l + 1)
            out = [[None] * blocks for _ in range(4)]
            for b in range(blocks):
                c = [state[l][f][b] for f in range(4)]
                q = stepped(
                    [base[f][b] for f in range(4)],
                    c,
                    [east(v) for v in c],
                    [west(v) for v in c],
                    [norths[f][b] for f in range(4)],
                    [souths[f][b] for f in range(4)],
                    [state[above][f][b] for f in range(4)],
                    [state[below][f][b] for f in range(4)],
                    scale,
                )
                for f in range(4):
                    out[f][b] = q[f] if f == 0 else jnp.where(open_at[l][b], q[f], 0.0)
            return out

        one = {}
        for l in range(-1, 3):
            got = advance(zero, zero[l], l, 1.0, nb + 1 if l in (0, 1) else nb)
            if l == -1:
                got = [[jnp.where(exists, v, 0.0) for v in row] for row in got]
            one[l] = got if l in (0, 1) else [row + blank for row in got]
        for l in range(2):
            base = [
                [0.5 * (zero[l][f][b] + one[l][f][b]) for b in range(nb)] for f in range(4)
            ]
            two = advance(one, base, l, 0.5, nb)
            slot = 2 + l if side == 0 else 1 - l
            for b in range(nb):
                for f in range(4):
                    turned[b, pl.ds(f * 32 + slot, 8, stride=4), :] = two[f][b]
                sums[b] = sums[b] + (1.0 - jnp.exp(two[0][b] * (-0.125)))
    for b in range(nb):
        zp[b * LANES : (b + 1) * LANES, :] = turned[b].T

    per = x_n // count_z
    scale = 8.0 / math.sqrt(h_n * LANES * count_z)
    for b in range(nb):
        path[b] = sums[b] * scale
    for b in range(nb):
        own[:, blk[b]] = path[b, pl.ds(gz * per, per), :]
        for k in range(1, count_z):
            sends[k - 1][:, blk[b]] = path[b, pl.ds((gz ^ k) * per, per), :]


def write_kernel(dims, s2, zp, yp, o0, o1, o2, o3, buf, sem):
    x_n, h_n, ny = dims
    lane = lane_iota()
    sub = lax.broadcasted_iota(jnp.int32, (8, LANES), 0)
    outs = (o0, o1, o2, o3)
    tiles = ny // 8
    copies = []
    for f in range(4):
        for x in range(x_n):
            shift = (LANES - ((f * x_n + x) * 4 + 2)) % LANES

            def tile(t, carry, f=f, x=x, shift=shift):
                y = pl.multiple_of(t * 8, 8)
                edge = pltpu.roll(zp[pl.ds(y, 8), :], shift, 1)
                for h in range(h_n):
                    cols = slice(h * LANES, (h + 1) * LANES)
                    v = s2[f, x, pl.ds(y, 8), cols]
                    if h == 0:
                        v = jnp.where(lane < 2, edge, v)
                    if h == h_n - 1:
                        v = jnp.where(lane >= LANES - 2, edge, v)
                    buf[f, x, pl.ds(y, 8), cols] = v
                return carry

            for t in range(tiles):
                tile(t, 0)
            for side in range(2):
                t = 0 if side == 0 else tiles - 1
                for h in range(h_n):
                    cols = slice(h * LANES, (h + 1) * LANES)
                    v = buf[f, x, t * 8 : t * 8 + 8, cols]
                    for r in range(2):
                        at = r if side == 0 else 7 - r
                        row = yp[side * 8 + r * 4 + f, x : x + 1, cols]
                        keep = sub == at
                        if h == 0:
                            keep = keep & (lane >= 2)
                        if h == h_n - 1:
                            keep = keep & (lane < LANES - 2)
                        v = jnp.where(keep, row, v)
                    buf[f, x, t * 8 : t * 8 + 8, cols] = v
        copy = pltpu.make_async_copy(buf.at[f], outs[f], sem.at[f])
        copy.start()
        copies.append(copy)
    for c in copies:
        c.wait()


def pairs_of(count, wrap):
    a = [(i, i ^ 1) for i in range(count)]
    b = [(i, (i + 1) % count if i % 2 else (i - 1) % count) for i in range(count)]
    if not wrap:
        b = [(i, j) for i, j in b if abs(i - j) == 1]
    return a, b


def params(limit=LIMIT):
    return pltpu.CompilerParams(vmem_limit_bytes=limit)


def on_device(theta, u, v, w, markers):
    x_n, ny, nz = theta.shape
    h_n = nz // LANES
    count_z, count_y = lax.axis_size("gz"), lax.axis_size("gy")
    dims = (x_n, h_n, ny)
    nyp = ny + 2 * PAD
    f32 = jnp.float32
    fields = pltpu.VMEM((4, x_n, h_n, nyp, LANES), f32)
    args = [pltpu.with_memory_space_constraint(a, pltpu.HBM) for a in (theta, u, v, w, markers)]
    cells = x_n * ny * nz

    def cost(flops, moved):
        return pl.CostEstimate(flops=flops, bytes_accessed=moved, transcendentals=0)

    s0, mk, ys_a, ys_b, zown = pl.pallas_call(
        functools.partial(pack_kernel, dims),
        out_shape=(
            fields,
            pltpu.VMEM((x_n, h_n, nyp, LANES), jnp.int32),
            jax.ShapeDtypeStruct((72, nz), f32),
            jax.ShapeDtypeStruct((72, nz), f32),
            jax.ShapeDtypeStruct((2, 152, ny), f32),
        ),
        in_specs=[HBM] * 5,
        out_specs=(VMEM,) * 5,
        scratch_shapes=[
            pltpu.VMEM((3, ny, LANES), f32),
            pltpu.VMEM((3, ny // LANES, LANES, LANES), f32),
            pltpu.SemaphoreType.DMA((5, h_n)),
        ],
        compiler_params=params(),
        name="load_and_pack",
    )(*args)

    y_pairs = pairs_of(count_y, True)
    ya = lax.ppermute(ys_a, "gy", y_pairs[0])
    yb = lax.ppermute(ys_b, "gy", y_pairs[1])

    s1 = pl.pallas_call(
        functools.partial(section_one_kernel, dims),
        out_shape=fields,
        in_specs=[VMEM] * 2,
        out_specs=VMEM,
        compiler_params=params(),
        cost_estimate=cost(100 * cells, 36 * cells),
        name="section_one",
    )(s0, mk)

    zs_a, zs_b = pl.pallas_call(
        functools.partial(corner_kernel, dims),
        out_shape=(jax.ShapeDtypeStruct((104, ny), f32),) * 2,
        in_specs=[VMEM] * 3,
        out_specs=(VMEM,) * 2,
        compiler_params=params(),
        name="corners",
    )(ya, yb, zown)

    z_pairs = pairs_of(count_z, False)
    za = lax.ppermute(zs_a, "gz", z_pairs[0])
    zb = lax.ppermute(zs_b, "gz", z_pairs[1])

    s2, path = pl.pallas_call(
        functools.partial(section_two_kernel, dims),
        out_shape=(pltpu.VMEM((4, x_n, ny, nz), f32), jax.ShapeDtypeStruct((x_n, ny), f32)),
        in_specs=[VMEM] * 3,
        out_specs=(VMEM,) * 2,
        scratch_shapes=[pltpu.VMEM((x_n, ny, LANES), f32)],
        compiler_params=params(),
        cost_estimate=cost(110 * cells, 52 * cells),
        name="section_two",
    )(s0, mk, s1)

    per = x_n // count_z
    edges = pl.pallas_call(
        functools.partial(edge_kernel, dims, count_z),
        out_shape=(
            jax.ShapeDtypeStruct((ny, LANES), f32),
            jax.ShapeDtypeStruct((16, 8, nz), f32),
        )
        + (jax.ShapeDtypeStruct((per, ny), f32),) * count_z,
        in_specs=[VMEM] * 9,
        out_specs=(VMEM,) * (2 + count_z),
        scratch_shapes=[
            pltpu.VMEM((ny // LANES, LANES, LANES), f32),
            pltpu.VMEM((ny // LANES, 8, LANES), f32),
        ],
        compiler_params=params(),
        name="edges",
    )(s0, mk, s1, zown, ya, yb, za, zb, path)
    zp, yp, own = edges[:3]

    got = [
        lax.ppermute(part, "gz", [(i, i ^ k) for i in range(count_z)])
        for k, part in enumerate(edges[3:], start=1)
    ]

    outs = pl.pallas_call(
        functools.partial(write_kernel, dims),
        out_shape=(pltpu.HBM((x_n, ny, nz), f32),) * 4,
        in_specs=[VMEM] * 3,
        out_specs=(HBM,) * 4,
        scratch_shapes=[pltpu.VMEM((4, x_n, ny, nz), f32), pltpu.SemaphoreType.DMA((4,))],
        compiler_params=params(),
        cost_estimate=cost(cells, 32 * cells),
        name="write",
    )(s2, zp, yp)

    total = own
    for part in got:
        total = total + part
    return (*outs, total)


def solution(mesh):
    spec = P(None, "gy", "gz")
    return jax.shard_map(
        on_device,
        mesh=mesh,
        in_specs=(spec,) * 5,
        out_specs=(spec,) * 4 + (P("gz", "gy"),),
        check_vma=False,
    )
```

```python
import functools
import math

import jax
import jax.numpy as jnp
from jax import lax
from jax.experimental import pallas as pl
from jax.experimental.pallas import tpu as pltpu
from jax.sharding import PartitionSpec as P

TIME_STEP = 0.1
NU_BASE = 0.05
KAPPA_BASE = 0.05
SMAG_COEF = 0.03
PRANDTL = 0.4
BUOYANCY = 0.5
LANES = 128
PAD = 8
LIMIT = 16 << 20
HBM = pl.BlockSpec(memory_space=pltpu.HBM)
VMEM = pl.BlockSpec(memory_space=pltpu.VMEM)


def lane_iota():
    return lax.broadcasted_iota(jnp.int32, (8, LANES), 1)


def stepped(base, c, e, w, n, s, u, l, scale):
    h = TIME_STEP * scale
    dx = [a - b for a, b in zip(e, w)]
    dy = [a - b for a, b in zip(n, s)]
    dz = [a - b for a, b in zip(u, l)]
    lap = [
        ((a + b) + (p + q)) + ((r + t) - 6.0 * m)
        for a, b, p, q, r, t, m in zip(e, w, n, s, u, l, c)
    ]
    straight = dx[1] * dx[1] + dy[2] * dy[2] + dz[3] * dz[3]
    shear_a = dy[1] + dx[2]
    shear_b = dz[1] + dx[3]
    shear_c = dz[2] + dy[3]
    shear = shear_a * shear_a + shear_b * shear_b + shear_c * shear_c
    k = (SMAG_COEF * h) ** 2
    arg = (straight + straight + shear) * (0.25 * k) + 0.01 * k
    eddy = arg * lax.rsqrt(arg)
    c_mom = eddy + NU_BASE * h
    c_heat = eddy * (1.0 / PRANDTL) + KAPPA_BASE * h
    vel = [(0.5 * h) * q for q in c[1:]]
    out = []
    for i in range(4):
        coef = c_heat if i == 0 else c_mom
        adv = vel[0] * dx[i] + vel[1] * dy[i] + vel[2] * dz[i]
        out.append((base[i] + coef * lap[i]) - adv)
    out[3] = out[3] + (BUOYANCY * h) * c[0]
    return out


def lane_next(blocks, lane):
    r = [pltpu.roll(b, LANES - 1, 1) for b in blocks]
    if len(r) == 1:
        return r
    return [jnp.where(lane == LANES - 1, r[(i + 1) % len(r)], r[i]) for i in range(len(r))]


def lane_prev(blocks, lane):
    r = [pltpu.roll(b, 1, 1) for b in blocks]
    if len(r) == 1:
        return r
    return [jnp.where(lane == 0, r[i - 1], r[i]) for i in range(len(r))]


def height_pair(blocks, lane):
    count = len(blocks)
    up = [pltpu.roll(b, LANES - 1, 1) for b in blocks]
    lo = [pltpu.roll(b, 1, 1) for b in blocks]
    upper = [
        up[i] if i == count - 1 else jnp.where(lane == LANES - 1, up[i + 1], up[i])
        for i in range(count)
    ]
    lower = [lo[i] if i == 0 else jnp.where(lane == 0, lo[i - 1], lo[i]) for i in range(count)]
    return upper, lower


def east(q):
    return pltpu.roll(q, 7, 0)


def west(q):
    return pltpu.roll(q, 1, 0)


def flat(ref):
    return ref.reshape(math.prod(ref.shape[:-1]), LANES)


def row_of(ref, lead, x_stride, start, x):
    return ref[pl.ds(lead + start, x, stride=x_stride), :]


def pack_kernel(dims, *refs):
    x_n, h_n, ny = dims
    ins = refs[:5]
    s0, mk, ys_a, ys_b, zown, part, turned, sem = refs[5:]
    nyp = ny + 2 * PAD
    lane = lane_iota()
    copies = []
    for f in range(5):
        for h in range(h_n):
            dst = s0.at[f] if f < 4 else mk
            copies.append(
                pltpu.make_async_copy(
                    ins[f].at[:, :, pl.ds(h * LANES, LANES)],
                    dst.at[:, h, pl.ds(PAD, ny), :],
                    sem.at[f, h],
                )
            )
    for c in copies:
        c.start()
    even = lax.rem(lax.axis_index("gy"), 2) == 0
    s0_flat, mk_flat = flat(s0), flat(mk)
    stride = h_n * nyp
    group = lane // 8

    def arrived(f):
        for c in copies[f * h_n : (f + 1) * h_n]:
            c.wait()

    def pack_columns(a):
        def tile(t, carry):
            y = pl.multiple_of(PAD + t * 8, 8)
            yo = pl.multiple_of(t * 8, 8)
            acc = jnp.zeros((8, LANES), jnp.float32)
            for g in range(16 if a < 2 else 8):
                f, x = a * 2 + g // 8, g % 8
                if a < 2:
                    lo, hi = s0[f, x, 0, pl.ds(y, 8), :], s0[f, x, h_n - 1, pl.ds(y, 8), :]
                else:
                    lo, hi = mk[x, 0, pl.ds(y, 8), :], mk[x, h_n - 1, pl.ds(y, 8), :]
                both = jnp.where(lane < LANES // 2, lo, hi).astype(jnp.float32)
                acc = jnp.where(group == g, pltpu.roll(both, (g * 8 + 4) % LANES, 1), acc)
            part[a, pl.ds(yo, 8), :] = acc
            return carry

        lax.fori_loop(0, ny // 8, tile, 0, unroll=4)
        for b in range(ny // LANES):
            turned[a, b] = part[a, b * LANES : (b + 1) * LANES, :].T

    def rows(dst, ys):
        for r, y in enumerate(ys):
            for h in range(h_n):
                cols = slice(h * LANES, (h + 1) * LANES)
                for f in range(4):
                    block = row_of(s0_flat, (f * x_n * h_n + h) * nyp, stride, PAD + y, x_n)
                    dst[(r * 4 + f) * 8 : (r * 4 + f) * 8 + 8, cols] = block
                if r == 0:
                    block = row_of(mk_flat, h * nyp, stride, PAD + y, x_n)
                    dst[64:72, cols] = block.astype(jnp.float32)

    for a, fields in enumerate(((0, 1), (2, 3), (4,))):
        for f in fields:
            arrived(f)
        pack_columns(a)

    first, last = (0, 1), (ny - 1, ny - 2)

    @pl.when(even)
    def _():
        rows(ys_a, last)
        rows(ys_b, first)

    @pl.when(jnp.logical_not(even))
    def _():
        rows(ys_a, first)
        rows(ys_b, last)

    for side in range(2):
        for l in range(4):
            j = 4 + l if side == 0 else 3 - l
            for b in range(ny // LANES):
                cols = slice(b * LANES, (b + 1) * LANES)
                for f in range(4):
                    k = f * 4 + l
                    zown[side, k * 8 : k * 8 + 8, cols] = turned[
                        f // 2, b, pl.ds((f % 2) * 64 + j, 8, stride=8), :
                    ]
                if l < 3:
                    k = 16 + l
                    zown[side, k * 8 : k * 8 + 8, cols] = turned[2, b, pl.ds(j, 8, stride=8), :]


def y_halo(even, a_ref, b_ref, k, cols):
    a, b = a_ref[k * 8 : k * 8 + 8, cols], b_ref[k * 8 : k * 8 + 8, cols]
    return jnp.where(even, b, a), jnp.where(even, a, b)


def beyond(lane, even, ya, yb, h_n, side, f, l, rows):
    h = 0 if side == 0 else h_n - 1
    at = l if side == 0 else LANES - 1 - l
    out = jnp.zeros((8, LANES), jnp.float32)
    for r in rows:
        k = r * 4 + f if f < 4 else 8
        before, after = y_halo(even, ya, yb, k, slice(h * LANES, (h + 1) * LANES))
        out = jnp.where(
            lane == LANES - 1 - r, pltpu.roll(before, (LANES - 1 - r - at) % LANES, 1), out
        )
        out = jnp.where(lane == r, pltpu.roll(after, (r - at) % LANES, 1), out)
    return out


def corner_kernel(dims, ya, yb, zown, after, zs_a, zs_b):
    del after
    x_n, h_n, ny = dims
    lane = lane_iota()
    even = lax.rem(lax.axis_index("gy"), 2) == 0
    even_z = lax.rem(lax.axis_index("gz"), 2) == 0

    def strip(dst, side):
        for l in range(2):
            for f in range(4):
                k, m = l * 4 + f, f * 4 + l
                dst[k * 8 : k * 8 + 8, :] = zown[side, m * 8 : m * 8 + 8, :]
        dst[64:72, :] = zown[side, 128:136, :]
        for f in range(4):
            dst[72 + f * 8 : 80 + f * 8, 0:LANES] = beyond(
                lane, even, ya, yb, h_n, side, f, 0, (0,)
            )
            if ny > LANES:
                dst[72 + f * 8 : 80 + f * 8, LANES:] = jnp.zeros((8, ny - LANES), jnp.float32)

    @pl.when(even_z)
    def _():
        strip(zs_a, 1)
        strip(zs_b, 0)

    @pl.when(jnp.logical_not(even_z))
    def _():
        strip(zs_a, 0)
        strip(zs_b, 1)


def load4(ref, x, h, y):
    return [ref[f, x, h, pl.ds(y, 8), :] for f in range(4)]


def section_one_kernel(dims, s0, mk, s1):
    x_n, h_n, ny = dims
    lane = lane_iota()

    def tile(y, x):
        c = [load4(s0, x, h, y) for h in range(h_n)]
        pairs = [height_pair([c[h][f] for h in range(h_n)], lane) for f in range(4)]
        for h in range(h_n):
            r = stepped(
                c[h],
                c[h],
                load4(s0, (x + 1) % x_n, h, y),
                load4(s0, (x - 1) % x_n, h, y),
                load4(s0, x, h, y + 1),
                load4(s0, x, h, y - 1),
                [p[0][h] for p in pairs],
                [p[1][h] for p in pairs],
                1.0,
            )
            open_cell = mk[x, h, pl.ds(y, 8), :] != 0
            s1[0, x, h, pl.ds(y, 8), :] = r[0]
            for f in range(1, 4):
                s1[f, x, h, pl.ds(y, 8), :] = jnp.where(open_cell, r[f], 0.0)

    def body(t, carry):
        for j in range(2):
            y = pl.multiple_of(PAD + t * 16 + j * 8, 8)
            for x in range(x_n):
                tile(y, x)
        return carry

    lax.fori_loop(0, ny // 16, body, 0)


def section_two_kernel(dims, s0, mk, s1, s2, path, acc):
    x_n, h_n, ny = dims
    lane = lane_iota()
    sub = lax.broadcasted_iota(jnp.int32, (8, LANES), 0)

    def tile(y, yo, x):
        c = [load4(s1, x, h, y) for h in range(h_n)]
        pairs = [height_pair([c[h][f] for h in range(h_n)], lane) for f in range(4)]
        total = None
        for h in range(h_n):
            start = load4(s0, x, h, y)
            r = stepped(
                [0.5 * (a + b) for a, b in zip(start, c[h])],
                c[h],
                load4(s1, (x + 1) % x_n, h, y),
                load4(s1, (x - 1) % x_n, h, y),
                load4(s1, x, h, y + 1),
                load4(s1, x, h, y - 1),
                [p[0][h] for p in pairs],
                [p[1][h] for p in pairs],
                0.5,
            )
            open_cell = mk[x, h, pl.ds(y, 8), :] != 0
            cols = slice(h * LANES, (h + 1) * LANES)
            s2[0, x, pl.ds(yo, 8), cols] = r[0]
            for f in range(1, 4):
                s2[f, x, pl.ds(yo, 8), cols] = jnp.where(open_cell, r[f], 0.0)
            refr = 1.0 - jnp.exp(r[0] * (-0.125))
            if h == 0:
                refr = jnp.where(lane < 2, 0.0, refr)
            if h == h_n - 1:
                refr = jnp.where(lane >= LANES - 2, 0.0, refr)
            total = refr if total is None else total + refr
        return total

    def body(t, carry):
        for j in range(2):
            y = pl.multiple_of(PAD + t * 16 + j * 8, 8)
            yo = pl.multiple_of(t * 16 + j * 8, 8)
            for x in range(x_n):
                acc[x, pl.ds(yo, 8), :] = tile(y, yo, x)
        return carry

    lax.fori_loop(0, ny // 16, body, 0)
    ones = jnp.ones((LANES, LANES), jnp.bfloat16)
    diagonal = lax.broadcasted_iota(jnp.int32, (LANES, LANES), 0) == lax.broadcasted_iota(
        jnp.int32, (LANES, LANES), 1
    )
    for b in range(ny // LANES):
        cols = slice(b * LANES, (b + 1) * LANES)
        rows = jnp.concatenate([acc[x, cols, :] for x in range(x_n)], axis=0)
        high = rows.astype(jnp.bfloat16)
        rest = (rows - high.astype(jnp.float32)).astype(jnp.bfloat16)
        sums = jnp.dot(high, ones, preferred_element_type=jnp.float32)
        sums = sums + jnp.dot(rest, ones, preferred_element_type=jnp.float32)
        for x in range(x_n):
            one = jnp.where(diagonal, sums[x * LANES : (x + 1) * LANES], 0.0)
            path[x : x + 1, cols] = jnp.sum(one, axis=0, keepdims=True)


def edge_kernel(dims, count_z, *refs):
    x_n, h_n, ny = dims
    s0, mk, s1, zown, ya, yb, za, zb, path_in = refs[:9]
    zp, yp, own = refs[9:12]
    sends = refs[12 : 12 + count_z - 1]
    turned, path = refs[12 + count_z - 1 :]
    nyp = ny + 2 * PAD
    nb = ny // LANES
    lane = lane_iota()
    even = lax.rem(lax.axis_index("gy"), 2) == 0
    gz = lax.axis_index("gz")
    even_z = lax.rem(gz, 2) == 0
    s0_flat, s1_flat, mk_flat = flat(s0), flat(s1), flat(mk)
    stride = h_n * nyp
    blk = [slice(b * LANES, (b + 1) * LANES) for b in range(max(nb, h_n))]

    y_sums = []
    for side in range(2):

        def at(r):
            return PAD + (r if side == 0 else ny - 1 - r)

        def own_rows(ref, r):
            return [
                [row_of(ref, (f * x_n * h_n + h) * nyp, stride, at(r), x_n) for h in range(h_n)]
                for f in range(4)
            ]

        def halo(k):
            return [y_halo(even, ya, yb, k, blk[h])[side] for h in range(h_n)]

        zero = {
            -2: [halo(4 + f) for f in range(4)],
            -1: [halo(f) for f in range(4)],
        }
        for r in range(3):
            zero[r] = own_rows(s0_flat, r)
        open_at = {-1: [m != 0.0 for m in halo(8)]}
        for r in range(2):
            open_at[r] = [
                row_of(mk_flat, h * nyp, stride, at(r), x_n) != 0 for h in range(h_n)
            ]
        one = {r: own_rows(s1_flat, r) for r in (1, 2)}

        def advance(state, base, r, scale, fields=4):
            pairs = [height_pair(state[r][f], lane) for f in range(4)]
            ahead, behind = (r + 1, r - 1) if side == 0 else (r - 1, r + 1)
            out = [[None] * h_n for _ in range(4)]
            for h in range(h_n):
                c = [state[r][f][h] for f in range(4)]
                q = stepped(
                    [base[f][h] for f in range(4)],
                    c,
                    [east(v) for v in c],
                    [west(v) for v in c],
                    [state[ahead][f][h] for f in range(4)],
                    [state[behind][f][h] for f in range(4)],
                    [p[0][h] for p in pairs],
                    [p[1][h] for p in pairs],
                    scale,
                )
                for f in range(4):
                    out[f][h] = q[f] if f == 0 else jnp.where(open_at[r][h], q[f], 0.0)
            return out

        for r in (-1, 0):
            one[r] = advance(zero, zero[r], r, 1.0)
        for r in (0, 1):
            base = [
                [0.5 * (zero[r][f][h] + one[r][f][h]) for h in range(h_n)] for f in range(4)
            ]
            two = advance(one, base, r, 0.5)
            for f in range(4):
                for h in range(h_n):
                    yp[side * 8 + r * 4 + f, :, blk[h]] = two[f][h]
            total = None
            for h in range(h_n):
                refr = 1.0 - jnp.exp(two[0][h] * (-0.125))
                if h == 0:
                    refr = jnp.where(lane < 2, 0.0, refr)
                if h == h_n - 1:
                    refr = jnp.where(lane >= LANES - 2, 0.0, refr)
                total = refr if total is None else total + refr
            y_sums.append((r if side == 0 else ny - 1 - r, jnp.sum(total, axis=1, keepdims=True)))

    sums = [path_in[:, blk[b]] for b in range(nb)]
    for y, value in y_sums:
        b = y // LANES
        sums[b] = jnp.where(lane == y % LANES, value, sums[b])

    for side in range(2):
        exists = (gz > 0) if side == 0 else (gz < count_z - 1)

        def halo(k):
            cols = [slice(b * LANES, (b + 1) * LANES) for b in range(nb)]
            rows = slice(k * 8, k * 8 + 8)
            take_a = jnp.logical_not(even_z) if side == 0 else even_z
            got = [jnp.where(take_a, za[rows, c], zb[rows, c]) for c in cols]
            return [jnp.where(exists, v, 0.0) for v in got]

        def mine(k):
            return [zown[side, k * 8 : k * 8 + 8, blk[b]] for b in range(nb)]

        def extra(f, l, rows):
            return [beyond(lane, even, ya, yb, h_n, side, f, l, rows)]

        blank = [jnp.zeros((8, LANES), jnp.float32)]
        zero = {
            -2: [halo(4 + f) + blank for f in range(4)],
            -1: [halo(f) + halo(9 + f)[:1] for f in range(4)],
        }
        for l in range(4):
            zero[l] = [
                mine(f * 4 + l) + (extra(f, l, (0, 1)) if l < 3 else blank) for f in range(4)
            ]
        open_at = {-1: [m != 0.0 for m in halo(8)]}
        for l in range(3):
            open_at[l] = [m != 0.0 for m in mine(16 + l)]
        for l in range(2):
            open_at[l] = open_at[l] + [extra(4, l, (0,))[0] != 0.0]

        def advance(state, base, l, scale, blocks):
            norths = [lane_next(state[l][f], lane) for f in range(4)]
            souths = [lane_prev(state[l][f], lane) for f in range(4)]
            above, below = (l + 1, l - 1) if side == 0 else (l - 1, l + 1)
            out = [[None] * blocks for _ in range(4)]
            for b in range(blocks):
                c = [state[l][f][b] for f in range(4)]
                q = stepped(
                    [base[f][b] for f in range(4)],
                    c,
                    [east(v) for v in c],
                    [west(v) for v in c],
                    [norths[f][b] for f in range(4)],
                    [souths[f][b] for f in range(4)],
                    [state[above][f][b] for f in range(4)],
                    [state[below][f][b] for f in range(4)],
                    scale,
                )
                for f in range(4):
                    out[f][b] = q[f] if f == 0 else jnp.where(open_at[l][b], q[f], 0.0)
            return out

        one = {}
        for l in range(-1, 3):
            got = advance(zero, zero[l], l, 1.0, nb + 1 if l in (0, 1) else nb)
            if l == -1:
                got = [[jnp.where(exists, v, 0.0) for v in row] for row in got]
            one[l] = got if l in (0, 1) else [row + blank for row in got]
        for l in range(2):
            base = [
                [0.5 * (zero[l][f][b] + one[l][f][b]) for b in range(nb)] for f in range(4)
            ]
            two = advance(one, base, l, 0.5, nb)
            slot = 2 + l if side == 0 else 1 - l
            for b in range(nb):
                for f in range(4):
                    turned[b, pl.ds(f * 32 + slot, 8, stride=4), :] = two[f][b]
                sums[b] = sums[b] + (1.0 - jnp.exp(two[0][b] * (-0.125)))
    for b in range(nb):
        zp[b * LANES : (b + 1) * LANES, :] = turned[b].T

    per = x_n // count_z
    scale = 8.0 / math.sqrt(h_n * LANES * count_z)
    for b in range(nb):
        path[b] = sums[b] * scale
    for b in range(nb):
        own[:, blk[b]] = path[b, pl.ds(gz * per, per), :]
        for k in range(1, count_z):
            sends[k - 1][:, blk[b]] = path[b, pl.ds((gz ^ k) * per, per), :]


def write_kernel(dims, s2, zp, yp, *refs):
    x_n, h_n, ny = dims
    outs, (buf, sem) = refs[:4], refs[4:]
    lane = lane_iota()
    sub = lax.broadcasted_iota(jnp.int32, (8, LANES), 0)
    tiles = ny // 8
    copies = []
    for f in range(4):
        for x in range(x_n):
            shift = (LANES - ((f * x_n + x) * 4 + 2)) % LANES

            def tile(t, f=f, x=x, shift=shift):
                y = t * 8
                edge = pltpu.roll(zp[pl.ds(y, 8), :], shift, 1)
                for h in range(h_n):
                    cols = slice(h * LANES, (h + 1) * LANES)
                    v = s2[f, x, pl.ds(y, 8), cols]
                    if h == 0:
                        v = jnp.where(lane < 2, edge, v)
                    if h == h_n - 1:
                        v = jnp.where(lane >= LANES - 2, edge, v)
                    buf[f, x, pl.ds(y, 8), cols] = v

            for t in range(tiles):
                tile(t)
            for side in range(2):
                t = 0 if side == 0 else tiles - 1
                for h in range(h_n):
                    cols = slice(h * LANES, (h + 1) * LANES)
                    v = buf[f, x, t * 8 : t * 8 + 8, cols]
                    for r in range(2):
                        at = r if side == 0 else 7 - r
                        row = yp[side * 8 + r * 4 + f, x : x + 1, cols]
                        keep = sub == at
                        if h == 0:
                            keep = keep & (lane >= 2)
                        if h == h_n - 1:
                            keep = keep & (lane < LANES - 2)
                        v = jnp.where(keep, row, v)
                    buf[f, x, t * 8 : t * 8 + 8, cols] = v
        copy = pltpu.make_async_copy(buf.at[f], outs[f], sem.at[f])
        copy.start()
        copies.append(copy)
    for c in copies:
        c.wait()


def pairs_of(count):
    a = [(i, i ^ 1) for i in range(count)]
    b = [(i, (i + 1) % count if i % 2 else (i - 1) % count) for i in range(count)]
    return a, b


def inner_pairs(count_z, count_y):
    pairs = []
    for z, other in pairs_of(count_z)[1]:
        for y in range(count_y):
            to = other * count_y + y if abs(z - other) == 1 else z * count_y + (y ^ 1)
            pairs.append((z * count_y + y, to))
    return pairs


def params(limit=LIMIT):
    return pltpu.CompilerParams(vmem_limit_bytes=limit)


def on_device(theta, u, v, w, markers):
    x_n, ny, nz = theta.shape
    h_n = nz // LANES
    count_z, count_y = lax.axis_size("gz"), lax.axis_size("gy")
    dims = (x_n, h_n, ny)
    nyp = ny + 2 * PAD
    f32 = jnp.float32
    fields = pltpu.VMEM((4, x_n, h_n, nyp, LANES), f32)
    args = [pltpu.with_memory_space_constraint(a, pltpu.HBM) for a in (theta, u, v, w, markers)]
    cells = x_n * ny * nz

    def cost(flops, moved):
        return pl.CostEstimate(flops=flops, bytes_accessed=moved, transcendentals=0)

    s0, mk, ys_a, ys_b, zown = pl.pallas_call(
        functools.partial(pack_kernel, dims),
        out_shape=(
            fields,
            pltpu.VMEM((x_n, h_n, nyp, LANES), jnp.int32),
            jax.ShapeDtypeStruct((72, nz), f32),
            jax.ShapeDtypeStruct((72, nz), f32),
            jax.ShapeDtypeStruct((2, 152, ny), f32),
        ),
        in_specs=[HBM] * 5,
        out_specs=(VMEM,) * 5,
        scratch_shapes=[
            pltpu.VMEM((3, ny, LANES), f32),
            pltpu.VMEM((3, ny // LANES, LANES, LANES), f32),
            pltpu.SemaphoreType.DMA((5, h_n)),
        ],
        compiler_params=params(),
        name="load_and_pack",
    )(*args)

    y_pairs = pairs_of(count_y)
    ya = lax.ppermute(ys_a, "gy", y_pairs[0])
    yb = lax.ppermute(ys_b, "gy", y_pairs[1])

    s1 = pl.pallas_call(
        functools.partial(section_one_kernel, dims),
        out_shape=fields,
        in_specs=[VMEM] * 2,
        out_specs=VMEM,
        compiler_params=params(),
        cost_estimate=cost(100 * cells, 36 * cells),
        name="section_one",
    )(s0, mk)

    zs_a, zs_b = pl.pallas_call(
        functools.partial(corner_kernel, dims),
        out_shape=(jax.ShapeDtypeStruct((104, ny), f32),) * 2,
        in_specs=[VMEM] * 4,
        out_specs=(VMEM,) * 2,
        compiler_params=params(),
        name="corners",
    )(ya, yb, zown, s1)

    za = lax.ppermute(zs_a, "gz", pairs_of(count_z)[0])
    zb = lax.ppermute(zs_b, ("gz", "gy"), inner_pairs(count_z, count_y))

    s2, path = pl.pallas_call(
        functools.partial(section_two_kernel, dims),
        out_shape=(pltpu.VMEM((4, x_n, ny, nz), f32), jax.ShapeDtypeStruct((x_n, ny), f32)),
        in_specs=[VMEM] * 3,
        out_specs=(VMEM,) * 2,
        scratch_shapes=[pltpu.VMEM((x_n, ny, LANES), f32)],
        compiler_params=params(),
        cost_estimate=cost(110 * cells, 52 * cells),
        name="section_two",
    )(s0, mk, s1)

    per, nb = x_n // count_z, ny // LANES
    edges = pl.pallas_call(
        functools.partial(edge_kernel, dims, count_z),
        out_shape=(
            jax.ShapeDtypeStruct((ny, LANES), f32),
            jax.ShapeDtypeStruct((16, 8, nz), f32),
        )
        + (jax.ShapeDtypeStruct((per, ny), f32),) * count_z,
        in_specs=[VMEM] * 9,
        out_specs=(VMEM,) * (2 + count_z),
        scratch_shapes=[
            pltpu.VMEM((nb, LANES, LANES), f32),
            pltpu.VMEM((nb, x_n, LANES), f32),
        ],
        compiler_params=params(),
        name="edges",
    )(s0, mk, s1, zown, ya, yb, za, zb, path)
    zp, yp, own = edges[:3]

    total = own
    for k in range(count_z - 1, 0, -1):
        total = total + lax.ppermute(
            edges[2 + k], "gz", [(i, i ^ k) for i in range(count_z)]
        )

    outs = pl.pallas_call(
        functools.partial(write_kernel, dims),
        out_shape=(pltpu.HBM((x_n, ny, nz), f32),) * 4,
        in_specs=[VMEM] * 3,
        out_specs=(HBM,) * 4,
        scratch_shapes=[pltpu.VMEM((4, x_n, ny, nz), f32), pltpu.SemaphoreType.DMA((4,))],
        compiler_params=params(),
        cost_estimate=cost(cells, 32 * cells),
        name="write",
    )(s2, zp, yp)
    return (*outs, total)


def solution(mesh):
    spec = P(None, "gy", "gz")
    return jax.shard_map(
        on_device,
        mesh=mesh,
        in_specs=(spec,) * 5,
        out_specs=(spec,) * 4 + (P("gz", "gy"),),
        check_vma=False,
    )
```

```python
import functools
import math

import jax
import jax.numpy as jnp
from jax import lax
from jax.experimental import pallas as pl
from jax.experimental.pallas import tpu as pltpu
from jax.sharding import PartitionSpec as P

TIME_STEP = 0.1
NU_BASE = 0.05
KAPPA_BASE = 0.05
SMAG_COEF = 0.03
PRANDTL = 0.4
BUOYANCY = 0.5
LANES = 128
PAD = 8
LIMIT = 16 << 20
HBM = pl.BlockSpec(memory_space=pltpu.HBM)
VMEM = pl.BlockSpec(memory_space=pltpu.VMEM)


def lane_iota():
    return lax.broadcasted_iota(jnp.int32, (8, LANES), 1)


def stepped(base, c, e, w, n, s, u, l, scale):
    h = TIME_STEP * scale
    dx = [a - b for a, b in zip(e, w)]
    dy = [a - b for a, b in zip(n, s)]
    dz = [a - b for a, b in zip(u, l)]
    lap = [
        ((a + b) + (p + q)) + ((r + t) - 6.0 * m)
        for a, b, p, q, r, t, m in zip(e, w, n, s, u, l, c)
    ]
    straight = dx[1] * dx[1] + dy[2] * dy[2] + dz[3] * dz[3]
    shear_a = dy[1] + dx[2]
    shear_b = dz[1] + dx[3]
    shear_c = dz[2] + dy[3]
    shear = shear_a * shear_a + shear_b * shear_b + shear_c * shear_c
    k = (SMAG_COEF * h) ** 2
    arg = (straight + straight + shear) * (0.25 * k) + 0.01 * k
    eddy = arg * lax.rsqrt(arg)
    c_mom = eddy + NU_BASE * h
    c_heat = eddy * (1.0 / PRANDTL) + KAPPA_BASE * h
    vel = [(0.5 * h) * q for q in c[1:]]
    out = []
    for i in range(4):
        coef = c_heat if i == 0 else c_mom
        adv = vel[0] * dx[i] + vel[1] * dy[i] + vel[2] * dz[i]
        out.append((base[i] + coef * lap[i]) - adv)
    out[3] = out[3] + (BUOYANCY * h) * c[0]
    return out


def lane_next(blocks, lane):
    r = [pltpu.roll(b, LANES - 1, 1) for b in blocks]
    if len(r) == 1:
        return r
    return [jnp.where(lane == LANES - 1, r[(i + 1) % len(r)], r[i]) for i in range(len(r))]


def lane_prev(blocks, lane):
    r = [pltpu.roll(b, 1, 1) for b in blocks]
    if len(r) == 1:
        return r
    return [jnp.where(lane == 0, r[i - 1], r[i]) for i in range(len(r))]


def height_pair(blocks, lane):
    count = len(blocks)
    up = [pltpu.roll(b, LANES - 1, 1) for b in blocks]
    lo = [pltpu.roll(b, 1, 1) for b in blocks]
    upper = [
        up[i] if i == count - 1 else jnp.where(lane == LANES - 1, up[i + 1], up[i])
        for i in range(count)
    ]
    lower = [lo[i] if i == 0 else jnp.where(lane == 0, lo[i - 1], lo[i]) for i in range(count)]
    return upper, lower


def east(q):
    return pltpu.roll(q, 7, 0)


def west(q):
    return pltpu.roll(q, 1, 0)


def flat(ref):
    return ref.reshape(math.prod(ref.shape[:-1]), LANES)


def row_of(ref, lead, x_stride, start, x):
    return ref[pl.ds(lead + start, x, stride=x_stride), :]


def pack_kernel(dims, parts, *refs):
    x_n, h_n, ny = dims
    ins = refs[:5]
    s0, mk, ys_a, ys_b, zown, part, turned, sem = refs[5:]
    nyp = ny + 2 * PAD
    lane = lane_iota()
    sub = lax.broadcasted_iota(jnp.int32, (8, LANES), 0)
    size = ny // parts
    copies = []
    for p in range(parts):
        for f in range(5):
            for h in range(h_n):
                dst = s0.at[f] if f < 4 else mk
                copies.append(
                    pltpu.make_async_copy(
                        ins[f].at[:, pl.ds(p * size, size), pl.ds(h * LANES, LANES)],
                        dst.at[:, h, pl.ds(PAD + p * size, size), :],
                        sem.at[p, f, h],
                    )
                )
    for c in copies:
        c.start()
    group = lane // 8

    def columns(t):
        y = PAD + t * 8
        for a in range(2):
            acc = jnp.zeros((8, LANES), jnp.float32)
            for g in range(16):
                f, x = a * 2 + g // 8, g % 8
                lo, hi = s0[f, x, 0, pl.ds(y, 8), :], s0[f, x, h_n - 1, pl.ds(y, 8), :]
                both = jnp.where(lane < LANES // 2, lo, hi)
                acc = jnp.where(group == g, pltpu.roll(both, (g * 8 + 4) % LANES, 1), acc)
            part[a, pl.ds(t * 8, 8), :] = acc
        bits = jnp.zeros((8, LANES), jnp.int32)
        for x in range(x_n):
            lo, hi = mk[x, 0, pl.ds(y, 8), :], mk[x, h_n - 1, pl.ds(y, 8), :]
            bits = bits + jnp.where(lane < LANES // 2, lo, hi) * (1 << x)
        part[2, pl.ds(t * 8, 8), :] = bits.astype(jnp.float32)

    for p in range(parts):
        for c in copies[p * 5 * h_n : (p + 1) * 5 * h_n]:
            c.wait()
        for t in range(p * size // 8, (p + 1) * size // 8):
            columns(t)

    even = lax.rem(lax.axis_index("gy"), 2) == 0
    s0_flat, mk_flat = flat(s0), flat(mk)
    stride = h_n * nyp
    for h in range(h_n):
        cols = slice(h * LANES, (h + 1) * LANES)
        for k in range(9):
            r, f = k // 4 % 2, k % 4

            def row(y):
                if k == 8:
                    return row_of(mk_flat, h * nyp, stride, PAD + y, x_n).astype(jnp.float32)
                return row_of(s0_flat, (f * x_n * h_n + h) * nyp, stride, PAD + y, x_n)

            first, last = row(r), row(ny - 1 - r)
            ys_a[k * 8 : k * 8 + 8, cols] = jnp.where(even, last, first)
            ys_b[k * 8 : k * 8 + 8, cols] = jnp.where(even, first, last)

    bit = jnp.zeros((8, LANES), jnp.int32)
    for x in range(x_n):
        bit = jnp.where(sub == x, 1 << x, bit)
    for b in range(ny // LANES):
        cols = slice(b * LANES, (b + 1) * LANES)
        for a in range(3):
            turned[a, b] = part[a, cols, :].T
        for side in range(2):
            for l in range(4):
                j = 4 + l if side == 0 else 3 - l
                for f in range(4):
                    k = f * 4 + l
                    zown[side, k * 8 : k * 8 + 8, cols] = turned[
                        f // 2, b, pl.ds((f % 2) * 64 + j, 8, stride=8), :
                    ]
                if l < 3:
                    k, at = 16 + l, l if side == 0 else LANES - 1 - l
                    row = jnp.broadcast_to(turned[2, b, at : at + 1, :], (8, LANES))
                    has = jnp.bitwise_and(row.astype(jnp.int32), bit) != 0
                    zown[side, k * 8 : k * 8 + 8, cols] = jnp.where(has, 1.0, 0.0)


def y_halo(even, a_ref, b_ref, k, cols):
    a, b = a_ref[k * 8 : k * 8 + 8, cols], b_ref[k * 8 : k * 8 + 8, cols]
    return jnp.where(even, b, a), jnp.where(even, a, b)


def beyond(lane, even, ya, yb, h_n, side, f, l, rows):
    h = 0 if side == 0 else h_n - 1
    at = l if side == 0 else LANES - 1 - l
    out = jnp.zeros((8, LANES), jnp.float32)
    for r in rows:
        k = r * 4 + f if f < 4 else 8
        before, after = y_halo(even, ya, yb, k, slice(h * LANES, (h + 1) * LANES))
        out = jnp.where(
            lane == LANES - 1 - r, pltpu.roll(before, (LANES - 1 - r - at) % LANES, 1), out
        )
        out = jnp.where(lane == r, pltpu.roll(after, (r - at) % LANES, 1), out)
    return out


def corner_kernel(dims, yb, ya, zown, after, zs_a, zs_b):
    del after
    x_n, h_n, ny = dims
    lane = lane_iota()
    even = lax.rem(lax.axis_index("gy"), 2) == 0
    even_z = lax.rem(lax.axis_index("gz"), 2) == 0

    def strip(dst, side):
        for l in range(2):
            for f in range(4):
                k, m = l * 4 + f, f * 4 + l
                dst[k * 8 : k * 8 + 8, :] = zown[side, m * 8 : m * 8 + 8, :]
        dst[64:72, :] = zown[side, 128:136, :]
        for f in range(4):
            dst[72 + f * 8 : 80 + f * 8, 0:LANES] = beyond(
                lane, even, ya, yb, h_n, side, f, 0, (0,)
            )
            if ny > LANES:
                dst[72 + f * 8 : 80 + f * 8, LANES:] = jnp.zeros((8, ny - LANES), jnp.float32)

    @pl.when(even_z)
    def _():
        strip(zs_a, 1)
        strip(zs_b, 0)

    @pl.when(jnp.logical_not(even_z))
    def _():
        strip(zs_a, 0)
        strip(zs_b, 1)


def load4(ref, x, h, y):
    return [ref[f, x, h, pl.ds(y, 8), :] for f in range(4)]


def section_one_kernel(dims, s0, mk, s1):
    x_n, h_n, ny = dims
    lane = lane_iota()

    def tile(y, x):
        c = [load4(s0, x, h, y) for h in range(h_n)]
        pairs = [height_pair([c[h][f] for h in range(h_n)], lane) for f in range(4)]
        for h in range(h_n):
            r = stepped(
                c[h],
                c[h],
                load4(s0, (x + 1) % x_n, h, y),
                load4(s0, (x - 1) % x_n, h, y),
                load4(s0, x, h, y + 1),
                load4(s0, x, h, y - 1),
                [p[0][h] for p in pairs],
                [p[1][h] for p in pairs],
                1.0,
            )
            open_cell = mk[x, h, pl.ds(y, 8), :] != 0
            s1[0, x, h, pl.ds(y, 8), :] = r[0]
            for f in range(1, 4):
                s1[f, x, h, pl.ds(y, 8), :] = jnp.where(open_cell, r[f], 0.0)

    def body(t, carry):
        for j in range(4):
            y = pl.multiple_of(PAD + t * 32 + j * 8, 8)
            for x in range(x_n):
                tile(y, x)
        return carry

    lax.fori_loop(0, ny // 32, body, 0)


def outer_rows(dims, s0, mk, ya, yb, s1):
    x_n, h_n, ny = dims
    nyp = ny + 2 * PAD
    lane = lane_iota()
    even = lax.rem(lax.axis_index("gy"), 2) == 0
    s0_flat, s1_flat, mk_flat = flat(s0), flat(s1), flat(mk)
    stride = h_n * nyp
    blk = [slice(h * LANES, (h + 1) * LANES) for h in range(h_n)]
    for side in range(2):

        def start(f, h, r):
            return (f * x_n * h_n + h) * nyp + PAD + (r if side == 0 else ny - 1 - r)

        def halo(k):
            return [y_halo(even, ya, yb, k, blk[h])[side] for h in range(h_n)]

        zero = {-2: [halo(4 + f) for f in range(4)], -1: [halo(f) for f in range(4)]}
        for r in range(2):
            zero[r] = [
                [row_of(s0_flat, 0, stride, start(f, h, r), x_n) for h in range(h_n)]
                for f in range(4)
            ]
        open_at = {
            -1: [m != 0.0 for m in halo(8)],
            0: [row_of(mk_flat, 0, stride, start(0, h, 0), x_n) != 0 for h in range(h_n)],
        }
        for r in (-1, 0):
            pairs = [height_pair(zero[r][f], lane) for f in range(4)]
            ahead, behind = (r + 1, r - 1) if side == 0 else (r - 1, r + 1)
            for h in range(h_n):
                c = [zero[r][f][h] for f in range(4)]
                q = stepped(
                    c,
                    c,
                    [east(v) for v in c],
                    [west(v) for v in c],
                    [zero[ahead][f][h] for f in range(4)],
                    [zero[behind][f][h] for f in range(4)],
                    [p[0][h] for p in pairs],
                    [p[1][h] for p in pairs],
                    1.0,
                )
                for f in range(4):
                    v = q[f] if f == 0 else jnp.where(open_at[r][h], q[f], 0.0)
                    s1_flat[pl.ds(start(f, h, r), x_n, stride=stride), :] = v


def section_two_kernel(dims, s0, mk, s1_in, yb, ya, s2, path, s1, acc):
    del s1_in
    x_n, h_n, ny = dims
    lane = lane_iota()
    outer_rows(dims, s0, mk, ya, yb, s1)

    def tile(y, yo, x):
        c = [load4(s1, x, h, y) for h in range(h_n)]
        pairs = [height_pair([c[h][f] for h in range(h_n)], lane) for f in range(4)]
        total = None
        for h in range(h_n):
            start = load4(s0, x, h, y)
            r = stepped(
                [0.5 * (a + b) for a, b in zip(start, c[h])],
                c[h],
                load4(s1, (x + 1) % x_n, h, y),
                load4(s1, (x - 1) % x_n, h, y),
                load4(s1, x, h, y + 1),
                load4(s1, x, h, y - 1),
                [p[0][h] for p in pairs],
                [p[1][h] for p in pairs],
                0.5,
            )
            open_cell = mk[x, h, pl.ds(y, 8), :] != 0
            cols = slice(h * LANES, (h + 1) * LANES)
            s2[0, x, pl.ds(yo, 8), cols] = r[0]
            for f in range(1, 4):
                s2[f, x, pl.ds(yo, 8), cols] = jnp.where(open_cell, r[f], 0.0)
            refr = 1.0 - jnp.exp(r[0] * (-0.125))
            if h == 0:
                refr = jnp.where(lane < 2, 0.0, refr)
            if h == h_n - 1:
                refr = jnp.where(lane >= LANES - 2, 0.0, refr)
            total = refr if total is None else total + refr
        return total

    def body(t, carry):
        for j in range(4):
            y = pl.multiple_of(PAD + t * 32 + j * 8, 8)
            yo = pl.multiple_of(t * 32 + j * 8, 8)
            for x in range(x_n):
                acc[x, pl.ds(yo, 8), :] = tile(y, yo, x)
        return carry

    lax.fori_loop(0, ny // 32, body, 0)
    for x in range(x_n):
        for b in range(ny // LANES):
            cols = slice(b * LANES, (b + 1) * LANES)
            path[x : x + 1, cols] = jnp.sum(acc[x, cols, :].T, axis=0, keepdims=True)


def edge_kernel(dims, count_z, *refs):
    x_n, h_n, ny = dims
    zown, yb, ya, zb, za, path_in = refs[:6]
    zp, own = refs[6:8]
    sends = refs[8 : 8 + count_z - 1]
    turned, path = refs[8 + count_z - 1 :]
    nb = ny // LANES
    lane = lane_iota()
    even = lax.rem(lax.axis_index("gy"), 2) == 0
    gz = lax.axis_index("gz")
    even_z = lax.rem(gz, 2) == 0
    blk = [slice(b * LANES, (b + 1) * LANES) for b in range(nb)]

    sums = [path_in[:, blk[b]] for b in range(nb)]

    for side in range(2):
        exists = (gz > 0) if side == 0 else (gz < count_z - 1)

        def halo(k):
            cols = [slice(b * LANES, (b + 1) * LANES) for b in range(nb)]
            rows = slice(k * 8, k * 8 + 8)
            take_a = jnp.logical_not(even_z) if side == 0 else even_z
            got = [jnp.where(take_a, za[rows, c], zb[rows, c]) for c in cols]
            return [jnp.where(exists, v, 0.0) for v in got]

        def mine(k):
            return [zown[side, k * 8 : k * 8 + 8, blk[b]] for b in range(nb)]

        def extra(f, l, rows):
            return [beyond(lane, even, ya, yb, h_n, side, f, l, rows)]

        blank = [jnp.zeros((8, LANES), jnp.float32)]
        zero = {
            -2: [halo(4 + f) + blank for f in range(4)],
            -1: [halo(f) + halo(9 + f)[:1] for f in range(4)],
        }
        for l in range(4):
            zero[l] = [
                mine(f * 4 + l) + (extra(f, l, (0, 1)) if l < 3 else blank) for f in range(4)
            ]
        open_at = {-1: [m != 0.0 for m in halo(8)]}
        for l in range(3):
            open_at[l] = [m != 0.0 for m in mine(16 + l)]
        for l in range(2):
            open_at[l] = open_at[l] + [extra(4, l, (0,))[0] != 0.0]

        def advance(state, base, l, scale, blocks):
            norths = [lane_next(state[l][f], lane) for f in range(4)]
            souths = [lane_prev(state[l][f], lane) for f in range(4)]
            above, below = (l + 1, l - 1) if side == 0 else (l - 1, l + 1)
            out = [[None] * blocks for _ in range(4)]
            for b in range(blocks):
                c = [state[l][f][b] for f in range(4)]
                q = stepped(
                    [base[f][b] for f in range(4)],
                    c,
                    [east(v) for v in c],
                    [west(v) for v in c],
                    [norths[f][b] for f in range(4)],
                    [souths[f][b] for f in range(4)],
                    [state[above][f][b] for f in range(4)],
                    [state[below][f][b] for f in range(4)],
                    scale,
                )
                for f in range(4):
                    out[f][b] = q[f] if f == 0 else jnp.where(open_at[l][b], q[f], 0.0)
            return out

        one = {}
        for l in range(-1, 3):
            got = advance(zero, zero[l], l, 1.0, nb + 1 if l in (0, 1) else nb)
            if l == -1:
                got = [[jnp.where(exists, v, 0.0) for v in row] for row in got]
            one[l] = got if l in (0, 1) else [row + blank for row in got]
        for l in range(2):
            base = [
                [0.5 * (zero[l][f][b] + one[l][f][b]) for b in range(nb)] for f in range(4)
            ]
            two = advance(one, base, l, 0.5, nb)
            slot = 2 + l if side == 0 else 1 - l
            for b in range(nb):
                for f in range(4):
                    turned[b, pl.ds(f * 32 + slot, 8, stride=4), :] = two[f][b]
                sums[b] = sums[b] + (1.0 - jnp.exp(two[0][b] * (-0.125)))
    for b in range(nb):
        zp[b * LANES : (b + 1) * LANES, :] = turned[b].T

    per = x_n // count_z
    scale = 8.0 / math.sqrt(h_n * LANES * count_z)
    for b in range(nb):
        path[b] = sums[b] * scale
    for b in range(nb):
        own[:, blk[b]] = path[b, pl.ds(gz * per, per), :]
        for k in range(1, count_z):
            sends[k - 1][:, blk[b]] = path[b, pl.ds((gz ^ k) * per, per), :]


def write_kernel(dims, pieces, s2, zp, *refs):
    x_n, h_n, ny = dims
    outs, (buf, sem) = refs[:4], refs[4:]
    lane = lane_iota()
    size = x_n // pieces
    copies = []
    for f in range(4):
        for x in range(x_n):
            for t in range(ny // 8):
                rows = slice(t * 8, t * 8 + 8)
                edge = pltpu.roll(zp[rows, :], (LANES - ((f * x_n + x) * 4 + 2)) % LANES, 1)
                for h in range(h_n):
                    cols = slice(h * LANES, (h + 1) * LANES)
                    v = s2[f, x, rows, cols]
                    if h == 0:
                        v = jnp.where(lane < 2, edge, v)
                    if h == h_n - 1:
                        v = jnp.where(lane >= LANES - 2, edge, v)
                    buf[f, x, rows, cols] = v
            if (x + 1) % size == 0:
                part = pl.ds(x + 1 - size, size)
                copies.append(
                    pltpu.make_async_copy(buf.at[f, part], outs[f].at[part], sem.at[f, x // size])
                )
                copies[-1].start()
    for c in copies:
        c.wait()


def pairs_of(count):
    a = [(i, i ^ 1) for i in range(count)]
    b = [(i, (i + 1) % count if i % 2 else (i - 1) % count) for i in range(count)]
    return a, b


def inner_pairs(count_z, count_y):
    pairs = []
    for z, other in pairs_of(count_z)[1]:
        for y in range(count_y):
            to = other * count_y + y if abs(z - other) == 1 else z * count_y + (y ^ 1)
            pairs.append((z * count_y + y, to))
    return pairs


def params(limit=LIMIT):
    return pltpu.CompilerParams(vmem_limit_bytes=limit)


def on_device(theta, u, v, w, markers):
    x_n, ny, nz = theta.shape
    h_n = nz // LANES
    count_z, count_y = lax.axis_size("gz"), lax.axis_size("gy")
    dims = (x_n, h_n, ny)
    nyp = ny + 2 * PAD
    f32 = jnp.float32
    fields = pltpu.VMEM((4, x_n, h_n, nyp, LANES), f32)
    args = [pltpu.with_memory_space_constraint(a, pltpu.HBM) for a in (theta, u, v, w, markers)]
    cells = x_n * ny * nz

    def cost(flops, moved):
        return pl.CostEstimate(flops=flops, bytes_accessed=moved, transcendentals=0)

    s0, mk, ys_a, ys_b, zown = pl.pallas_call(
        functools.partial(pack_kernel, dims, 2),
        out_shape=(
            fields,
            pltpu.VMEM((x_n, h_n, nyp, LANES), jnp.int32),
            jax.ShapeDtypeStruct((72, nz), f32),
            jax.ShapeDtypeStruct((72, nz), f32),
            jax.ShapeDtypeStruct((2, 152, ny), f32),
        ),
        in_specs=[HBM] * 5,
        out_specs=(VMEM,) * 5,
        scratch_shapes=[
            pltpu.VMEM((3, ny, LANES), f32),
            pltpu.VMEM((3, ny // LANES, LANES, LANES), f32),
            pltpu.SemaphoreType.DMA((2, 5, h_n)),
        ],
        compiler_params=params(),
        name="load_and_pack",
    )(*args)

    y_pairs = pairs_of(count_y)
    yb = lax.ppermute(ys_b, "gy", y_pairs[1])
    ya = lax.ppermute(ys_a, "gy", y_pairs[0])

    s1 = pl.pallas_call(
        functools.partial(section_one_kernel, dims),
        out_shape=fields,
        in_specs=[VMEM] * 2,
        out_specs=VMEM,
        compiler_params=params(),
        cost_estimate=cost(100 * cells, 36 * cells),
        name="section_one",
    )(s0, mk)

    zs_a, zs_b = pl.pallas_call(
        functools.partial(corner_kernel, dims),
        out_shape=(jax.ShapeDtypeStruct((104, ny), f32),) * 2,
        in_specs=[VMEM] * 4,
        out_specs=(VMEM,) * 2,
        compiler_params=params(),
        name="corners",
    )(yb, ya, zown, s1)

    zb = lax.ppermute(zs_b, ("gz", "gy"), inner_pairs(count_z, count_y))
    za = lax.ppermute(zs_a, "gz", pairs_of(count_z)[0])

    s2, path, _ = pl.pallas_call(
        functools.partial(section_two_kernel, dims),
        out_shape=(
            pltpu.VMEM((4, x_n, ny, nz), f32),
            jax.ShapeDtypeStruct((x_n, ny), f32),
            fields,
        ),
        in_specs=[VMEM] * 5,
        out_specs=(VMEM,) * 3,
        input_output_aliases={2: 2},
        scratch_shapes=[pltpu.VMEM((x_n, ny, LANES), f32)],
        compiler_params=params(),
        cost_estimate=cost(110 * cells, 52 * cells),
        name="section_two",
    )(s0, mk, s1, yb, ya)

    per, nb = x_n // count_z, ny // LANES
    edges = pl.pallas_call(
        functools.partial(edge_kernel, dims, count_z),
        out_shape=(
            jax.ShapeDtypeStruct((ny, LANES), f32),
        )
        + (jax.ShapeDtypeStruct((per, ny), f32),) * count_z,
        in_specs=[VMEM] * 6,
        out_specs=(VMEM,) * (1 + count_z),
        scratch_shapes=[
            pltpu.VMEM((nb, LANES, LANES), f32),
            pltpu.VMEM((nb, x_n, LANES), f32),
        ],
        compiler_params=params(),
        name="edges",
    )(zown, yb, ya, zb, za, path)
    zp, own = edges[:2]

    total = own
    for k in range(count_z - 1, 0, -1):
        total = total + lax.ppermute(
            edges[1 + k], "gz", [(i, i ^ k) for i in range(count_z)]
        )

    outs = pl.pallas_call(
        functools.partial(write_kernel, dims, 4),
        out_shape=(pltpu.HBM((x_n, ny, nz), f32),) * 4,
        in_specs=[VMEM] * 2,
        out_specs=(HBM,) * 4,
        scratch_shapes=[pltpu.VMEM((4, x_n, ny, nz), f32), pltpu.SemaphoreType.DMA((4, 4))],
        compiler_params=params(),
        cost_estimate=cost(cells, 32 * cells),
        name="write",
    )(s2, zp)
    return (*outs, total)


def solution(mesh):
    spec = P(None, "gy", "gz")
    return jax.shard_map(
        on_device,
        mesh=mesh,
        in_specs=(spec,) * 5,
        out_specs=(spec,) * 4 + (P("gz", "gy"),),
        check_vma=False,
    )
```

```python
import functools
import math

import jax
import jax.numpy as jnp
from jax import lax
from jax.experimental import pallas as pl
from jax.experimental.pallas import tpu as pltpu
from jax.sharding import PartitionSpec as P

TIME_STEP = 0.1
NU_BASE = 0.05
KAPPA_BASE = 0.05
SMAG_COEF = 0.03
PRANDTL = 0.4
BUOYANCY = 0.5
LANES = 128
PAD = 8
LIMIT = 16 << 20
HBM = pl.BlockSpec(memory_space=pltpu.HBM)
VMEM = pl.BlockSpec(memory_space=pltpu.VMEM)


def lane_iota():
    return lax.broadcasted_iota(jnp.int32, (8, LANES), 1)


def stepped(base, c, e, w, n, s, u, l, scale):
    h = TIME_STEP * scale
    dx = [a - b for a, b in zip(e, w)]
    dy = [a - b for a, b in zip(n, s)]
    dz = [a - b for a, b in zip(u, l)]
    lap = [
        ((a + b) + (p + q)) + ((r + t) - 6.0 * m)
        for a, b, p, q, r, t, m in zip(e, w, n, s, u, l, c)
    ]
    straight = dx[1] * dx[1] + dy[2] * dy[2] + dz[3] * dz[3]
    shear_a = dy[1] + dx[2]
    shear_b = dz[1] + dx[3]
    shear_c = dz[2] + dy[3]
    shear = shear_a * shear_a + shear_b * shear_b + shear_c * shear_c
    k = (SMAG_COEF * h) ** 2
    arg = (straight + straight + shear) * (0.25 * k) + 0.01 * k
    eddy = arg * lax.rsqrt(arg)
    c_mom = eddy + NU_BASE * h
    c_heat = eddy * (1.0 / PRANDTL) + KAPPA_BASE * h
    vel = [(0.5 * h) * q for q in c[1:]]
    out = []
    for i in range(4):
        coef = c_heat if i == 0 else c_mom
        adv = vel[0] * dx[i] + vel[1] * dy[i] + vel[2] * dz[i]
        out.append((base[i] + coef * lap[i]) - adv)
    out[3] = out[3] + (BUOYANCY * h) * c[0]
    return out


def lane_next(blocks, lane):
    r = [pltpu.roll(b, LANES - 1, 1) for b in blocks]
    if len(r) == 1:
        return r
    return [jnp.where(lane == LANES - 1, r[(i + 1) % len(r)], r[i]) for i in range(len(r))]


def lane_prev(blocks, lane):
    r = [pltpu.roll(b, 1, 1) for b in blocks]
    if len(r) == 1:
        return r
    return [jnp.where(lane == 0, r[i - 1], r[i]) for i in range(len(r))]


def height_pair(blocks, lane):
    count = len(blocks)
    up = [pltpu.roll(b, LANES - 1, 1) for b in blocks]
    lo = [pltpu.roll(b, 1, 1) for b in blocks]
    upper = [
        up[i] if i == count - 1 else jnp.where(lane == LANES - 1, up[i + 1], up[i])
        for i in range(count)
    ]
    lower = [lo[i] if i == 0 else jnp.where(lane == 0, lo[i - 1], lo[i]) for i in range(count)]
    return upper, lower


def east(q):
    return pltpu.roll(q, 7, 0)


def west(q):
    return pltpu.roll(q, 1, 0)


def flat(ref):
    return ref.reshape(math.prod(ref.shape[:-1]), LANES)


def row_of(ref, lead, x_stride, start, x):
    return ref[pl.ds(lead + start, x, stride=x_stride), :]


def pack_kernel(dims, parts, *refs):
    x_n, h_n, ny = dims
    ins = refs[:5]
    s0, mk, ys_a, ys_b, zown, part, turned, sem = refs[5:]
    nyp = ny + 2 * PAD
    lane = lane_iota()
    sub = lax.broadcasted_iota(jnp.int32, (8, LANES), 0)
    size = ny // parts
    copies = []
    for p in range(parts):
        for f in range(5):
            for h in range(h_n):
                dst = s0.at[f] if f < 4 else mk
                copies.append(
                    pltpu.make_async_copy(
                        ins[f].at[:, pl.ds(p * size, size), pl.ds(h * LANES, LANES)],
                        dst.at[:, h, pl.ds(PAD + p * size, size), :],
                        sem.at[p, f, h],
                    )
                )
    for c in copies:
        c.start()
    group = lane // 8

    def columns(t):
        y = PAD + t * 8
        for a in range(2):
            acc = jnp.zeros((8, LANES), jnp.float32)
            for g in range(16):
                f, x = a * 2 + g // 8, g % 8
                lo, hi = s0[f, x, 0, pl.ds(y, 8), :], s0[f, x, h_n - 1, pl.ds(y, 8), :]
                both = jnp.where(lane < LANES // 2, lo, hi)
                acc = jnp.where(group == g, pltpu.roll(both, (g * 8 + 4) % LANES, 1), acc)
            part[a, pl.ds(t * 8, 8), :] = acc
        bits = jnp.zeros((8, LANES), jnp.int32)
        for x in range(x_n):
            lo, hi = mk[x, 0, pl.ds(y, 8), :], mk[x, h_n - 1, pl.ds(y, 8), :]
            bits = bits + jnp.where(lane < LANES // 2, lo, hi) * (1 << x)
        part[2, pl.ds(t * 8, 8), :] = bits.astype(jnp.float32)

    for p in range(parts):
        for c in copies[p * 5 * h_n : (p + 1) * 5 * h_n]:
            c.wait()
        for t in range(p * size // 8, (p + 1) * size // 8):
            columns(t)

    even = lax.rem(lax.axis_index("gy"), 2) == 0
    s0_flat, mk_flat = flat(s0), flat(mk)
    stride = h_n * nyp
    for h in range(h_n):
        cols = slice(h * LANES, (h + 1) * LANES)
        for k in range(9):
            r, f = k // 4 % 2, k % 4

            def row(y):
                if k == 8:
                    return row_of(mk_flat, h * nyp, stride, PAD + y, x_n).astype(jnp.float32)
                return row_of(s0_flat, (f * x_n * h_n + h) * nyp, stride, PAD + y, x_n)

            first, last = row(r), row(ny - 1 - r)
            ys_a[k * 8 : k * 8 + 8, cols] = jnp.where(even, last, first)
            ys_b[k * 8 : k * 8 + 8, cols] = jnp.where(even, first, last)

    bit = jnp.zeros((8, LANES), jnp.int32)
    for x in range(x_n):
        bit = jnp.where(sub == x, 1 << x, bit)
    for b in range(ny // LANES):
        cols = slice(b * LANES, (b + 1) * LANES)
        for a in range(3):
            turned[a, b] = part[a, cols, :].T
        for side in range(2):
            for l in range(4):
                j = 4 + l if side == 0 else 3 - l
                for f in range(4):
                    k = f * 4 + l
                    zown[side, k * 8 : k * 8 + 8, cols] = turned[
                        f // 2, b, pl.ds((f % 2) * 64 + j, 8, stride=8), :
                    ]
                if l < 3:
                    k, at = 16 + l, l if side == 0 else LANES - 1 - l
                    row = jnp.broadcast_to(turned[2, b, at : at + 1, :], (8, LANES))
                    has = jnp.bitwise_and(row.astype(jnp.int32), bit) != 0
                    zown[side, k * 8 : k * 8 + 8, cols] = jnp.where(has, 1.0, 0.0)


def y_halo(even, a_ref, b_ref, k, cols):
    a, b = a_ref[k * 8 : k * 8 + 8, cols], b_ref[k * 8 : k * 8 + 8, cols]
    return jnp.where(even, b, a), jnp.where(even, a, b)


def beyond(lane, even, ya, yb, h_n, side, f, l, rows):
    h = 0 if side == 0 else h_n - 1
    at = l if side == 0 else LANES - 1 - l
    out = jnp.zeros((8, LANES), jnp.float32)
    for r in rows:
        k = r * 4 + f if f < 4 else 8
        before, after = y_halo(even, ya, yb, k, slice(h * LANES, (h + 1) * LANES))
        out = jnp.where(
            lane == LANES - 1 - r, pltpu.roll(before, (LANES - 1 - r - at) % LANES, 1), out
        )
        out = jnp.where(lane == r, pltpu.roll(after, (r - at) % LANES, 1), out)
    return out


def corner_kernel(dims, yb, ya, zown, after, zs_a, zs_b):
    del after
    x_n, h_n, ny = dims
    lane = lane_iota()
    even = lax.rem(lax.axis_index("gy"), 2) == 0
    even_z = lax.rem(lax.axis_index("gz"), 2) == 0

    def strip(dst, side):
        for l in range(2):
            for f in range(4):
                k, m = l * 4 + f, f * 4 + l
                dst[k * 8 : k * 8 + 8, :] = zown[side, m * 8 : m * 8 + 8, :]
        dst[64:72, :] = zown[side, 128:136, :]
        for f in range(4):
            dst[72 + f * 8 : 80 + f * 8, 0:LANES] = beyond(
                lane, even, ya, yb, h_n, side, f, 0, (0,)
            )
            if ny > LANES:
                dst[72 + f * 8 : 80 + f * 8, LANES:] = jnp.zeros((8, ny - LANES), jnp.float32)

    @pl.when(even_z)
    def _():
        strip(zs_a, 1)
        strip(zs_b, 0)

    @pl.when(jnp.logical_not(even_z))
    def _():
        strip(zs_a, 0)
        strip(zs_b, 1)


def load4(ref, x, h, y):
    return [ref[f, x, h, pl.ds(y, 8), :] for f in range(4)]


def section_one_kernel(dims, s0, mk, s1):
    x_n, h_n, ny = dims
    lane = lane_iota()

    def tile(y, x):
        c = [load4(s0, x, h, y) for h in range(h_n)]
        pairs = [height_pair([c[h][f] for h in range(h_n)], lane) for f in range(4)]
        for h in range(h_n):
            r = stepped(
                c[h],
                c[h],
                load4(s0, (x + 1) % x_n, h, y),
                load4(s0, (x - 1) % x_n, h, y),
                load4(s0, x, h, y + 1),
                load4(s0, x, h, y - 1),
                [p[0][h] for p in pairs],
                [p[1][h] for p in pairs],
                1.0,
            )
            open_cell = mk[x, h, pl.ds(y, 8), :] != 0
            s1[0, x, h, pl.ds(y, 8), :] = r[0]
            for f in range(1, 4):
                s1[f, x, h, pl.ds(y, 8), :] = jnp.where(open_cell, r[f], 0.0)

    for t in range(ny // 8):
        for x in range(x_n):
            tile(PAD + t * 8, x)


def outer_rows(dims, s0, mk, ya, yb, s1):
    x_n, h_n, ny = dims
    nyp = ny + 2 * PAD
    lane = lane_iota()
    even = lax.rem(lax.axis_index("gy"), 2) == 0
    s0_flat, s1_flat, mk_flat = flat(s0), flat(s1), flat(mk)
    stride = h_n * nyp
    blk = [slice(h * LANES, (h + 1) * LANES) for h in range(h_n)]
    for side in range(2):

        def start(f, h, r):
            return (f * x_n * h_n + h) * nyp + PAD + (r if side == 0 else ny - 1 - r)

        def halo(k):
            return [y_halo(even, ya, yb, k, blk[h])[side] for h in range(h_n)]

        zero = {-2: [halo(4 + f) for f in range(4)], -1: [halo(f) for f in range(4)]}
        for r in range(2):
            zero[r] = [
                [row_of(s0_flat, 0, stride, start(f, h, r), x_n) for h in range(h_n)]
                for f in range(4)
            ]
        open_at = {
            -1: [m != 0.0 for m in halo(8)],
            0: [row_of(mk_flat, 0, stride, start(0, h, 0), x_n) != 0 for h in range(h_n)],
        }
        for r in (-1, 0):
            pairs = [height_pair(zero[r][f], lane) for f in range(4)]
            ahead, behind = (r + 1, r - 1) if side == 0 else (r - 1, r + 1)
            for h in range(h_n):
                c = [zero[r][f][h] for f in range(4)]
                q = stepped(
                    c,
                    c,
                    [east(v) for v in c],
                    [west(v) for v in c],
                    [zero[ahead][f][h] for f in range(4)],
                    [zero[behind][f][h] for f in range(4)],
                    [p[0][h] for p in pairs],
                    [p[1][h] for p in pairs],
                    1.0,
                )
                for f in range(4):
                    v = q[f] if f == 0 else jnp.where(open_at[r][h], q[f], 0.0)
                    s1_flat[pl.ds(start(f, h, r), x_n, stride=stride), :] = v


def section_two_kernel(dims, s0, mk, s1_in, yb, ya, s2, acc, s1):
    del s1_in
    x_n, h_n, ny = dims
    lane = lane_iota()

    def tile(y, yo, x):
        c = [load4(s1, x, h, y) for h in range(h_n)]
        pairs = [height_pair([c[h][f] for h in range(h_n)], lane) for f in range(4)]
        total = None
        for h in range(h_n):
            start = load4(s0, x, h, y)
            r = stepped(
                [0.5 * (a + b) for a, b in zip(start, c[h])],
                c[h],
                load4(s1, (x + 1) % x_n, h, y),
                load4(s1, (x - 1) % x_n, h, y),
                load4(s1, x, h, y + 1),
                load4(s1, x, h, y - 1),
                [p[0][h] for p in pairs],
                [p[1][h] for p in pairs],
                0.5,
            )
            open_cell = mk[x, h, pl.ds(y, 8), :] != 0
            cols = slice(h * LANES, (h + 1) * LANES)
            s2[0, x, pl.ds(yo, 8), cols] = r[0]
            for f in range(1, 4):
                s2[f, x, pl.ds(yo, 8), cols] = jnp.where(open_cell, r[f], 0.0)
            refr = 1.0 - jnp.exp(r[0] * (-0.125))
            if h == 0:
                refr = jnp.where(lane < 2, 0.0, refr)
            if h == h_n - 1:
                refr = jnp.where(lane >= LANES - 2, 0.0, refr)
            total = refr if total is None else total + refr
        return total

    def tiles(places):
        for t in places:
            for x in range(x_n):
                acc[x, t * 8 : t * 8 + 8, :] = tile(PAD + t * 8, t * 8, x)

    last = ny // 8 - 1
    tiles(range(1, last))
    outer_rows(dims, s0, mk, ya, yb, s1)
    tiles((0, last))


def lane_sums(acc, b):
    x_n = acc.shape[0]
    rows = acc[:, b * LANES : (b + 1) * LANES, :].reshape(x_n * LANES, LANES)
    ones = jnp.ones((LANES, LANES), jnp.bfloat16)
    total = None
    for _ in range(3):
        piece = rows.astype(jnp.bfloat16)
        rows = rows - piece.astype(jnp.float32)
        got = jnp.dot(piece, ones, preferred_element_type=jnp.float32)
        total = got if total is None else total + got
    shape = (LANES, LANES)
    diagonal = lax.broadcasted_iota(jnp.int32, shape, 0) == lax.broadcasted_iota(
        jnp.int32, shape, 1
    )
    sub = lax.broadcasted_iota(jnp.int32, (8, LANES), 0)
    out = jnp.zeros((8, LANES), jnp.float32)
    for x in range(x_n):
        part = jnp.where(diagonal, total[x * LANES : (x + 1) * LANES], 0.0)
        out = jnp.where(sub == x, jnp.sum(part, axis=0, keepdims=True), out)
    return out


def edge_kernel(dims, count_z, *refs):
    x_n, h_n, ny = dims
    zown, yb, ya, zb, za, acc = refs[:6]
    zp, own = refs[6:8]
    sends = refs[8 : 8 + count_z - 1]
    turned, path = refs[8 + count_z - 1 :]
    nb = ny // LANES
    lane = lane_iota()
    even = lax.rem(lax.axis_index("gy"), 2) == 0
    gz = lax.axis_index("gz")
    even_z = lax.rem(gz, 2) == 0
    blk = [slice(b * LANES, (b + 1) * LANES) for b in range(nb)]

    sums = [lane_sums(acc, b) for b in range(nb)]

    for side in range(2):
        exists = (gz > 0) if side == 0 else (gz < count_z - 1)

        def halo(k):
            cols = [slice(b * LANES, (b + 1) * LANES) for b in range(nb)]
            rows = slice(k * 8, k * 8 + 8)
            take_a = jnp.logical_not(even_z) if side == 0 else even_z
            got = [jnp.where(take_a, za[rows, c], zb[rows, c]) for c in cols]
            return [jnp.where(exists, v, 0.0) for v in got]

        def mine(k):
            return [zown[side, k * 8 : k * 8 + 8, blk[b]] for b in range(nb)]

        def extra(f, l, rows):
            return [beyond(lane, even, ya, yb, h_n, side, f, l, rows)]

        blank = [jnp.zeros((8, LANES), jnp.float32)]
        zero = {
            -2: [halo(4 + f) + blank for f in range(4)],
            -1: [halo(f) + halo(9 + f)[:1] for f in range(4)],
        }
        for l in range(4):
            zero[l] = [
                mine(f * 4 + l) + (extra(f, l, (0, 1)) if l < 3 else blank) for f in range(4)
            ]
        open_at = {-1: [m != 0.0 for m in halo(8)]}
        for l in range(3):
            open_at[l] = [m != 0.0 for m in mine(16 + l)]
        for l in range(2):
            open_at[l] = open_at[l] + [extra(4, l, (0,))[0] != 0.0]

        def advance(state, base, l, scale, blocks):
            norths = [lane_next(state[l][f], lane) for f in range(4)]
            souths = [lane_prev(state[l][f], lane) for f in range(4)]
            above, below = (l + 1, l - 1) if side == 0 else (l - 1, l + 1)
            out = [[None] * blocks for _ in range(4)]
            for b in range(blocks):
                c = [state[l][f][b] for f in range(4)]
                q = stepped(
                    [base[f][b] for f in range(4)],
                    c,
                    [east(v) for v in c],
                    [west(v) for v in c],
                    [norths[f][b] for f in range(4)],
                    [souths[f][b] for f in range(4)],
                    [state[above][f][b] for f in range(4)],
                    [state[below][f][b] for f in range(4)],
                    scale,
                )
                for f in range(4):
                    out[f][b] = q[f] if f == 0 else jnp.where(open_at[l][b], q[f], 0.0)
            return out

        one = {}
        for l in range(-1, 3):
            got = advance(zero, zero[l], l, 1.0, nb + 1 if l in (0, 1) else nb)
            if l == -1:
                got = [[jnp.where(exists, v, 0.0) for v in row] for row in got]
            one[l] = got if l in (0, 1) else [row + blank for row in got]
        for l in range(2):
            base = [
                [0.5 * (zero[l][f][b] + one[l][f][b]) for b in range(nb)] for f in range(4)
            ]
            two = advance(one, base, l, 0.5, nb)
            slot = 2 + l if side == 0 else 1 - l
            for b in range(nb):
                for f in range(4):
                    turned[b, pl.ds(f * 32 + slot, 8, stride=4), :] = two[f][b]
                sums[b] = sums[b] + (1.0 - jnp.exp(two[0][b] * (-0.125)))
    for b in range(nb):
        zp[b * LANES : (b + 1) * LANES, :] = turned[b].T

    per = x_n // count_z
    scale = 8.0 / math.sqrt(h_n * LANES * count_z)
    for b in range(nb):
        path[b] = sums[b] * scale
    for b in range(nb):
        own[:, blk[b]] = path[b, pl.ds(gz * per, per), :]
        for k in range(1, count_z):
            sends[k - 1][:, blk[b]] = path[b, pl.ds((gz ^ k) * per, per), :]


def write_kernel(dims, pieces, s2, zp, *refs):
    x_n, h_n, ny = dims
    outs, (buf, sem) = refs[:4], refs[4:]
    lane = lane_iota()
    size = x_n // pieces
    copies = []
    for f in range(4):
        for x in range(x_n):
            for t in range(ny // 8):
                rows = slice(t * 8, t * 8 + 8)
                edge = pltpu.roll(zp[rows, :], (LANES - ((f * x_n + x) * 4 + 2)) % LANES, 1)
                for h in range(h_n):
                    cols = slice(h * LANES, (h + 1) * LANES)
                    v = s2[f, x, rows, cols]
                    if h == 0:
                        v = jnp.where(lane < 2, edge, v)
                    if h == h_n - 1:
                        v = jnp.where(lane >= LANES - 2, edge, v)
                    buf[f, x, rows, cols] = v
            if (x + 1) % size == 0:
                part = pl.ds(x + 1 - size, size)
                copies.append(
                    pltpu.make_async_copy(buf.at[f, part], outs[f].at[part], sem.at[f, x // size])
                )
                copies[-1].start()
    for c in copies:
        c.wait()


def pairs_of(count):
    a = [(i, i ^ 1) for i in range(count)]
    b = [(i, (i + 1) % count if i % 2 else (i - 1) % count) for i in range(count)]
    return a, b


def inner_pairs(count_z, count_y):
    pairs = []
    for z, other in pairs_of(count_z)[1]:
        for y in range(count_y):
            to = other * count_y + y if abs(z - other) == 1 else z * count_y + (y ^ 1)
            pairs.append((z * count_y + y, to))
    return pairs


def params(limit=LIMIT):
    return pltpu.CompilerParams(vmem_limit_bytes=limit)


def on_device(theta, u, v, w, markers):
    x_n, ny, nz = theta.shape
    h_n = nz // LANES
    count_z, count_y = lax.axis_size("gz"), lax.axis_size("gy")
    dims = (x_n, h_n, ny)
    nyp = ny + 2 * PAD
    f32 = jnp.float32
    fields = pltpu.VMEM((4, x_n, h_n, nyp, LANES), f32)
    args = [pltpu.with_memory_space_constraint(a, pltpu.HBM) for a in (theta, u, v, w, markers)]
    cells = x_n * ny * nz

    def cost(flops, moved):
        return pl.CostEstimate(flops=flops, bytes_accessed=moved, transcendentals=0)

    s0, mk, ys_a, ys_b, zown = pl.pallas_call(
        functools.partial(pack_kernel, dims, 2),
        out_shape=(
            fields,
            pltpu.VMEM((x_n, h_n, nyp, LANES), jnp.int32),
            jax.ShapeDtypeStruct((72, nz), f32),
            jax.ShapeDtypeStruct((72, nz), f32),
            jax.ShapeDtypeStruct((2, 152, ny), f32),
        ),
        in_specs=[HBM] * 5,
        out_specs=(VMEM,) * 5,
        scratch_shapes=[
            pltpu.VMEM((3, ny, LANES), f32),
            pltpu.VMEM((3, ny // LANES, LANES, LANES), f32),
            pltpu.SemaphoreType.DMA((2, 5, h_n)),
        ],
        compiler_params=params(),
        name="load_and_pack",
    )(*args)

    y_pairs = pairs_of(count_y)
    yb = lax.ppermute(ys_b, "gy", y_pairs[1])
    ya = lax.ppermute(ys_a, "gy", y_pairs[0])

    s1 = pl.pallas_call(
        functools.partial(section_one_kernel, dims),
        out_shape=fields,
        in_specs=[VMEM] * 2,
        out_specs=VMEM,
        compiler_params=params(),
        cost_estimate=cost(100 * cells, 36 * cells),
        name="section_one",
    )(s0, mk)

    zs_a, zs_b = pl.pallas_call(
        functools.partial(corner_kernel, dims),
        out_shape=(jax.ShapeDtypeStruct((104, ny), f32),) * 2,
        in_specs=[VMEM] * 4,
        out_specs=(VMEM,) * 2,
        compiler_params=params(),
        name="corners",
    )(yb, ya, zown, s1)

    zb = lax.ppermute(zs_b, ("gz", "gy"), inner_pairs(count_z, count_y))
    za = lax.ppermute(zs_a, "gz", pairs_of(count_z)[0])

    s2, acc, _ = pl.pallas_call(
        functools.partial(section_two_kernel, dims),
        out_shape=(
            pltpu.VMEM((4, x_n, ny, nz), f32),
            pltpu.VMEM((x_n, ny, LANES), f32),
            fields,
        ),
        in_specs=[VMEM] * 5,
        out_specs=(VMEM,) * 3,
        input_output_aliases={2: 2},
        compiler_params=params(),
        cost_estimate=cost(110 * cells, 52 * cells),
        name="section_two",
    )(s0, mk, s1, yb, ya)

    per, nb = x_n // count_z, ny // LANES
    edges = pl.pallas_call(
        functools.partial(edge_kernel, dims, count_z),
        out_shape=(
            jax.ShapeDtypeStruct((ny, LANES), f32),
        )
        + (jax.ShapeDtypeStruct((per, ny), f32),) * count_z,
        in_specs=[VMEM] * 6,
        out_specs=(VMEM,) * (1 + count_z),
        scratch_shapes=[
            pltpu.VMEM((nb, LANES, LANES), f32),
            pltpu.VMEM((nb, x_n, LANES), f32),
        ],
        compiler_params=params(),
        name="edges",
    )(zown, yb, ya, zb, za, acc)
    zp, own = edges[:2]

    total = own
    for k in range(count_z - 1, 0, -1):
        total = total + lax.ppermute(
            edges[1 + k], "gz", [(i, i ^ k) for i in range(count_z)]
        )

    outs = pl.pallas_call(
        functools.partial(write_kernel, dims, 4),
        out_shape=(pltpu.HBM((x_n, ny, nz), f32),) * 4,
        in_specs=[VMEM] * 2,
        out_specs=(HBM,) * 4,
        scratch_shapes=[pltpu.VMEM((4, x_n, ny, nz), f32), pltpu.SemaphoreType.DMA((4, 4))],
        compiler_params=params(),
        cost_estimate=cost(cells, 32 * cells),
        name="write",
    )(s2, zp)
    return (*outs, total)


def solution(mesh):
    spec = P(None, "gy", "gz")
    return jax.shard_map(
        on_device,
        mesh=mesh,
        in_specs=(spec,) * 5,
        out_specs=(spec,) * 4 + (P("gz", "gy"),),
        check_vma=False,
    )
```

```python
import functools
import math

import jax
import jax.numpy as jnp
from jax import lax
from jax.experimental import pallas as pl
from jax.experimental.pallas import tpu as pltpu
from jax.sharding import PartitionSpec as P

TIME_STEP = 0.1
NU_BASE = 0.05
KAPPA_BASE = 0.05
SMAG_COEF = 0.03
PRANDTL = 0.4
BUOYANCY = 0.5
LANES = 128
PAD = 8
LIMIT = 16 << 20
HBM = pl.BlockSpec(memory_space=pltpu.HBM)
VMEM = pl.BlockSpec(memory_space=pltpu.VMEM)


def lane_iota():
    return lax.broadcasted_iota(jnp.int32, (8, LANES), 1)


def stepped(base, c, e, w, n, s, u, l, given=None):
    half = 0.5 * TIME_STEP
    given = given or {}
    dx = [a - b for a, b in zip(e, w)]
    dy = [a - b for a, b in zip(n, s)]
    dz = [given[f][0] if f in given else u[f] - l[f] for f in range(4)]
    lz = [given[f][1] if f in given else (u[f] + l[f]) - 6.0 * c[f] for f in range(4)]
    lap = [((a + b) + (p + q)) + t for a, b, p, q, t in zip(e, w, n, s, lz)]
    straight = dx[1] * dx[1] + dy[2] * dy[2] + dz[3] * dz[3]
    shear_a = dy[1] + dx[2]
    shear_b = dz[1] + dx[3]
    shear_c = dz[2] + dy[3]
    shear = shear_a * shear_a + shear_b * shear_b + shear_c * shear_c
    k = (2.0 * SMAG_COEF) ** 2
    arg = (straight + straight + shear) * (0.25 * k) + 0.01 * k
    eddy = arg * lax.rsqrt(arg)
    c_mom = eddy + 2.0 * NU_BASE
    c_heat = eddy * (1.0 / PRANDTL) + 2.0 * KAPPA_BASE
    out = []
    for f in range(4):
        rate = (c_heat if f == 0 else c_mom) * lap[f]
        rate = rate - (c[1] * dx[f] + c[2] * dy[f] + c[3] * dz[f])
        if f == 3:
            rate = rate + (c[0] if 2.0 * BUOYANCY == 1.0 else (2.0 * BUOYANCY) * c[0])
        out.append(base[f] + half * rate)
    return out


def bent(theta):
    return 1.0 - jnp.exp2(theta * (-0.125 * math.log2(math.e)))


def lane_next(blocks, lane):
    r = [pltpu.roll(b, LANES - 1, 1) for b in blocks]
    if len(r) == 1:
        return r
    return [jnp.where(lane == LANES - 1, r[(i + 1) % len(r)], r[i]) for i in range(len(r))]


def lane_prev(blocks, lane):
    r = [pltpu.roll(b, 1, 1) for b in blocks]
    if len(r) == 1:
        return r
    return [jnp.where(lane == 0, r[i - 1], r[i]) for i in range(len(r))]


def height_pair(blocks, lane):
    count = len(blocks)
    up = [pltpu.roll(b, LANES - 1, 1) for b in blocks]
    lo = [pltpu.roll(b, 1, 1) for b in blocks]
    upper = [
        up[i] if i == count - 1 else jnp.where(lane == LANES - 1, up[i + 1], up[i])
        for i in range(count)
    ]
    lower = [lo[i] if i == 0 else jnp.where(lane == 0, lo[i - 1], lo[i]) for i in range(count)]
    return upper, lower


def east(q):
    return pltpu.roll(q, 7, 0)


def west(q):
    return pltpu.roll(q, 1, 0)


def flat(ref):
    return ref.reshape(math.prod(ref.shape[:-1]), LANES)


def row_of(ref, lead, x_stride, start, x):
    return ref[pl.ds(lead + start, x, stride=x_stride), :]


def height_matrix(nz):
    i = lax.broadcasted_iota(jnp.int32, (nz, 2 * nz), 0)
    j = lax.broadcasted_iota(jnp.int32, (nz, 2 * nz), 1)
    d = jnp.where(j < nz, i - j, i - j + nz)
    one, next_one = jnp.where(d == 1, 1.0, 0.0), jnp.where(d == -1, 1.0, 0.0)
    out = jnp.where(j < nz, one - next_one, one + next_one - jnp.where(d == 0, 6.0, 0.0))
    return out.astype(jnp.bfloat16)


def height_differences(rows, matrix):
    high = rows.astype(jnp.bfloat16)
    rest = (rows - high.astype(jnp.float32)).astype(jnp.bfloat16)
    return jnp.dot(
        jnp.concatenate([high, rest], axis=1), matrix, preferred_element_type=jnp.float32
    )


def pack_kernel(dims, parts, *refs):
    x_n, h_n, ny = dims
    ins = refs[:5]
    s0, mk, ys_a, ys_b, zown, zd, part, turned, matrix, sem = refs[5:]
    nyp = ny + 2 * PAD
    lane = lane_iota()
    sub = lax.broadcasted_iota(jnp.int32, (8, LANES), 0)
    size = ny // parts
    copies = []
    for p in range(parts):
        for f in range(5):
            for h in range(h_n):
                dst = s0.at[f] if f < 4 else mk
                copies.append(
                    pltpu.make_async_copy(
                        ins[f].at[:, pl.ds(p * size, size), pl.ds(h * LANES, LANES)],
                        dst.at[:, h, pl.ds(PAD + p * size, size), :],
                        sem.at[p, f, h],
                    )
                )
    for c in copies:
        c.start()
    group = lane // 8

    nz = h_n * LANES
    once = height_matrix(nz)
    matrix[0:nz, :] = once
    matrix[nz:, :] = once

    def heights(p):
        rows = slice(PAD + p * size, PAD + (p + 1) * size)
        q = jnp.concatenate(
            [
                jnp.concatenate([s0[0, x, h, rows, :] for h in range(h_n)], axis=1)
                for x in range(x_n)
            ],
            axis=0,
        )
        got = height_differences(q, matrix[...])
        for x in range(x_n):
            for h in range(h_n):
                for n in range(2):
                    at = n * nz + h * LANES
                    zd[n, x, h, p * size : (p + 1) * size, :] = got[
                        x * size : (x + 1) * size, at : at + LANES
                    ]

    def columns(t):
        y = PAD + t * 8
        for a in range(2):
            acc = jnp.zeros((8, LANES), jnp.float32)
            for g in range(16):
                f, x = a * 2 + g // 8, g % 8
                lo, hi = s0[f, x, 0, pl.ds(y, 8), :], s0[f, x, h_n - 1, pl.ds(y, 8), :]
                both = jnp.where(lane < LANES // 2, lo, hi)
                acc = jnp.where(group == g, pltpu.roll(both, (g * 8 + 4) % LANES, 1), acc)
            part[a, pl.ds(t * 8, 8), :] = acc
        bits = jnp.zeros((8, LANES), jnp.int32)
        for x in range(x_n):
            lo, hi = mk[x, 0, pl.ds(y, 8), :], mk[x, h_n - 1, pl.ds(y, 8), :]
            bits = bits + jnp.where(lane < LANES // 2, lo, hi) * (1 << x)
        part[2, pl.ds(t * 8, 8), :] = bits.astype(jnp.float32)

    for p in range(parts):
        for c in copies[p * 5 * h_n : (p + 1) * 5 * h_n]:
            c.wait()
        for t in range(p * size // 8, (p + 1) * size // 8):
            columns(t)
        heights(p)

    even = lax.rem(lax.axis_index("gy"), 2) == 0
    s0_flat, mk_flat = flat(s0), flat(mk)
    stride = h_n * nyp
    for h in range(h_n):
        cols = slice(h * LANES, (h + 1) * LANES)
        for k in range(9):
            r, f = k // 4 % 2, k % 4

            def row(y):
                if k == 8:
                    return row_of(mk_flat, h * nyp, stride, PAD + y, x_n).astype(jnp.float32)
                return row_of(s0_flat, (f * x_n * h_n + h) * nyp, stride, PAD + y, x_n)

            first, last = row(r), row(ny - 1 - r)
            ys_a[k * 8 : k * 8 + 8, cols] = jnp.where(even, last, first)
            ys_b[k * 8 : k * 8 + 8, cols] = jnp.where(even, first, last)

    bit = jnp.zeros((8, LANES), jnp.int32)
    for x in range(x_n):
        bit = jnp.where(sub == x, 1 << x, bit)
    for b in range(ny // LANES):
        cols = slice(b * LANES, (b + 1) * LANES)
        for a in range(3):
            turned[a, b] = part[a, cols, :].T
        for side in range(2):
            for l in range(4):
                j = 4 + l if side == 0 else 3 - l
                for f in range(4):
                    k = f * 4 + l
                    zown[side, k * 8 : k * 8 + 8, cols] = turned[
                        f // 2, b, pl.ds((f % 2) * 64 + j, 8, stride=8), :
                    ]
                if l < 3:
                    k, at = 16 + l, l if side == 0 else LANES - 1 - l
                    row = jnp.broadcast_to(turned[2, b, at : at + 1, :], (8, LANES))
                    has = jnp.bitwise_and(row.astype(jnp.int32), bit) != 0
                    zown[side, k * 8 : k * 8 + 8, cols] = jnp.where(has, 1.0, 0.0)


def y_halo(even, a_ref, b_ref, k, cols):
    a, b = a_ref[k * 8 : k * 8 + 8, cols], b_ref[k * 8 : k * 8 + 8, cols]
    return jnp.where(even, b, a), jnp.where(even, a, b)


def beyond(lane, even, ya, yb, h_n, side, f, l, rows):
    h = 0 if side == 0 else h_n - 1
    at = l if side == 0 else LANES - 1 - l
    out = jnp.zeros((8, LANES), jnp.float32)
    for r in rows:
        k = r * 4 + f if f < 4 else 8
        before, after = y_halo(even, ya, yb, k, slice(h * LANES, (h + 1) * LANES))
        out = jnp.where(
            lane == LANES - 1 - r, pltpu.roll(before, (LANES - 1 - r - at) % LANES, 1), out
        )
        out = jnp.where(lane == r, pltpu.roll(after, (r - at) % LANES, 1), out)
    return out


def corner_kernel(dims, yb, ya, zown, after, zs_a, zs_b):
    del after
    x_n, h_n, ny = dims
    lane = lane_iota()
    even = lax.rem(lax.axis_index("gy"), 2) == 0
    even_z = lax.rem(lax.axis_index("gz"), 2) == 0

    def strip(dst, side):
        for l in range(2):
            for f in range(4):
                k, m = l * 4 + f, f * 4 + l
                dst[k * 8 : k * 8 + 8, :] = zown[side, m * 8 : m * 8 + 8, :]
        dst[64:72, :] = zown[side, 128:136, :]
        for f in range(4):
            dst[72 + f * 8 : 80 + f * 8, 0:LANES] = beyond(
                lane, even, ya, yb, h_n, side, f, 0, (0,)
            )
            if ny > LANES:
                dst[72 + f * 8 : 80 + f * 8, LANES:] = jnp.zeros((8, ny - LANES), jnp.float32)

    @pl.when(even_z)
    def _():
        strip(zs_a, 1)
        strip(zs_b, 0)

    @pl.when(jnp.logical_not(even_z))
    def _():
        strip(zs_a, 0)
        strip(zs_b, 1)


def load4(ref, x, h, y):
    return [ref[f, x, h, pl.ds(y, 8), :] for f in range(4)]


def section_one_kernel(dims, s0, mk, zd, s1):
    x_n, h_n, ny = dims
    lane = lane_iota()

    def tile(y, yo, x):
        c = [load4(s0, x, h, y) for h in range(h_n)]
        pairs = [None] + [height_pair([c[h][f] for h in range(h_n)], lane) for f in range(1, 4)]
        for h in range(h_n):
            r = stepped(
                c[h],
                c[h],
                load4(s0, (x + 1) % x_n, h, y),
                load4(s0, (x - 1) % x_n, h, y),
                load4(s0, x, h, y + 1),
                load4(s0, x, h, y - 1),
                [None] + [p[0][h] for p in pairs[1:]],
                [None] + [p[1][h] for p in pairs[1:]],
                {0: [zd[n, x, h, pl.ds(yo, 8), :] for n in range(2)]},
            )
            open_cell = mk[x, h, pl.ds(y, 8), :] != 0
            s1[0, x, h, pl.ds(y, 8), :] = r[0]
            for f in range(1, 4):
                s1[f, x, h, pl.ds(y, 8), :] = jnp.where(open_cell, r[f], 0.0)

    for t in range(ny // 8):
        for x in range(x_n):
            tile(PAD + t * 8, t * 8, x)


def outer_rows(dims, s0, mk, ya, yb, s1):
    x_n, h_n, ny = dims
    nyp = ny + 2 * PAD
    lane = lane_iota()
    even = lax.rem(lax.axis_index("gy"), 2) == 0
    s0_flat, s1_flat, mk_flat = flat(s0), flat(s1), flat(mk)
    stride = h_n * nyp
    blk = [slice(h * LANES, (h + 1) * LANES) for h in range(h_n)]
    for side in range(2):

        def start(f, h, r):
            return (f * x_n * h_n + h) * nyp + PAD + (r if side == 0 else ny - 1 - r)

        def halo(k):
            return [y_halo(even, ya, yb, k, blk[h])[side] for h in range(h_n)]

        zero = {-2: [halo(4 + f) for f in range(4)], -1: [halo(f) for f in range(4)]}
        for r in range(2):
            zero[r] = [
                [row_of(s0_flat, 0, stride, start(f, h, r), x_n) for h in range(h_n)]
                for f in range(4)
            ]
        open_at = {
            -1: [m != 0.0 for m in halo(8)],
            0: [row_of(mk_flat, 0, stride, start(0, h, 0), x_n) != 0 for h in range(h_n)],
        }
        for r in (-1, 0):
            pairs = [height_pair(zero[r][f], lane) for f in range(4)]
            ahead, behind = (r + 1, r - 1) if side == 0 else (r - 1, r + 1)
            for h in range(h_n):
                c = [zero[r][f][h] for f in range(4)]
                q = stepped(
                    c,
                    c,
                    [east(v) for v in c],
                    [west(v) for v in c],
                    [zero[ahead][f][h] for f in range(4)],
                    [zero[behind][f][h] for f in range(4)],
                    [p[0][h] for p in pairs],
                    [p[1][h] for p in pairs],
                )
                for f in range(4):
                    v = q[f] if f == 0 else jnp.where(open_at[r][h], q[f], 0.0)
                    s1_flat[pl.ds(start(f, h, r), x_n, stride=stride), :] = v


def section_two_kernel(dims, s0, mk, s1_in, yb, ya, s2, acc, s1):
    del s1_in
    x_n, h_n, ny = dims
    lane = lane_iota()

    def tile(y, yo, x):
        c = [load4(s1, x, h, y) for h in range(h_n)]
        pairs = [height_pair([c[h][f] for h in range(h_n)], lane) for f in range(4)]
        total = None
        for h in range(h_n):
            start = load4(s0, x, h, y)
            r = stepped(
                [a + b for a, b in zip(start, c[h])],
                c[h],
                load4(s1, (x + 1) % x_n, h, y),
                load4(s1, (x - 1) % x_n, h, y),
                load4(s1, x, h, y + 1),
                load4(s1, x, h, y - 1),
                [p[0][h] for p in pairs],
                [p[1][h] for p in pairs],
            )
            part = jnp.where(mk[x, h, pl.ds(y, 8), :] != 0, 0.5, 0.0)
            theta = 0.5 * r[0]
            cols = slice(h * LANES, (h + 1) * LANES)
            s2[0, x, pl.ds(yo, 8), cols] = theta
            for f in range(1, 4):
                s2[f, x, pl.ds(yo, 8), cols] = part * r[f]
            refr = bent(theta)
            if h == 0:
                refr = jnp.where(lane < 2, 0.0, refr)
            if h == h_n - 1:
                refr = jnp.where(lane >= LANES - 2, 0.0, refr)
            total = refr if total is None else total + refr
        return total

    def tiles(places):
        for t in places:
            for x in range(x_n):
                acc[x, t * 8 : t * 8 + 8, :] = tile(PAD + t * 8, t * 8, x)

    last = ny // 8 - 1
    tiles(range(1, last))
    outer_rows(dims, s0, mk, ya, yb, s1)
    tiles((0, last))


def lane_sums(acc, b):
    x_n = acc.shape[0]
    rows = acc[:, b * LANES : (b + 1) * LANES, :].reshape(x_n * LANES, LANES)
    ones = jnp.ones((LANES, LANES), jnp.bfloat16)
    total = None
    for _ in range(3):
        piece = rows.astype(jnp.bfloat16)
        rows = rows - piece.astype(jnp.float32)
        got = jnp.dot(piece, ones, preferred_element_type=jnp.float32)
        total = got if total is None else total + got
    shape = (LANES, LANES)
    diagonal = lax.broadcasted_iota(jnp.int32, shape, 0) == lax.broadcasted_iota(
        jnp.int32, shape, 1
    )
    sub = lax.broadcasted_iota(jnp.int32, (8, LANES), 0)
    out = jnp.zeros((8, LANES), jnp.float32)
    for x in range(x_n):
        part = jnp.where(diagonal, total[x * LANES : (x + 1) * LANES], 0.0)
        out = jnp.where(sub == x, jnp.sum(part, axis=0, keepdims=True), out)
    return out


def edge_kernel(dims, count_z, *refs):
    x_n, h_n, ny = dims
    zown, yb, ya, zb, za, acc = refs[:6]
    zp, own = refs[6:8]
    sends = refs[8 : 8 + count_z - 1]
    turned, path = refs[8 + count_z - 1 :]
    nb = ny // LANES
    lane = lane_iota()
    even = lax.rem(lax.axis_index("gy"), 2) == 0
    gz = lax.axis_index("gz")
    even_z = lax.rem(gz, 2) == 0
    blk = [slice(b * LANES, (b + 1) * LANES) for b in range(nb)]

    sums = [lane_sums(acc, b) for b in range(nb)]

    for side in range(2):
        exists = (gz > 0) if side == 0 else (gz < count_z - 1)

        def halo(k):
            cols = [slice(b * LANES, (b + 1) * LANES) for b in range(nb)]
            rows = slice(k * 8, k * 8 + 8)
            take_a = jnp.logical_not(even_z) if side == 0 else even_z
            got = [jnp.where(take_a, za[rows, c], zb[rows, c]) for c in cols]
            return [jnp.where(exists, v, 0.0) for v in got]

        def mine(k):
            return [zown[side, k * 8 : k * 8 + 8, blk[b]] for b in range(nb)]

        def extra(f, l, rows):
            return [beyond(lane, even, ya, yb, h_n, side, f, l, rows)]

        blank = [jnp.zeros((8, LANES), jnp.float32)]
        zero = {
            -2: [halo(4 + f) + blank for f in range(4)],
            -1: [halo(f) + halo(9 + f)[:1] for f in range(4)],
        }
        for l in range(4):
            zero[l] = [
                mine(f * 4 + l) + (extra(f, l, (0, 1)) if l < 3 else blank) for f in range(4)
            ]
        open_at = {-1: [m != 0.0 for m in halo(8)]}
        for l in range(3):
            open_at[l] = [m != 0.0 for m in mine(16 + l)]
        for l in range(2):
            open_at[l] = open_at[l] + [extra(4, l, (0,))[0] != 0.0]

        def advance(state, base, l, blocks):
            norths = [lane_next(state[l][f], lane) for f in range(4)]
            souths = [lane_prev(state[l][f], lane) for f in range(4)]
            above, below = (l + 1, l - 1) if side == 0 else (l - 1, l + 1)
            out = [[None] * blocks for _ in range(4)]
            for b in range(blocks):
                c = [state[l][f][b] for f in range(4)]
                q = stepped(
                    [base[f][b] for f in range(4)],
                    c,
                    [east(v) for v in c],
                    [west(v) for v in c],
                    [norths[f][b] for f in range(4)],
                    [souths[f][b] for f in range(4)],
                    [state[above][f][b] for f in range(4)],
                    [state[below][f][b] for f in range(4)],
                )
                for f in range(4):
                    out[f][b] = q[f] if f == 0 else jnp.where(open_at[l][b], q[f], 0.0)
            return out

        one = {}
        for l in range(-1, 3):
            got = advance(zero, zero[l], l, nb + 1 if l in (0, 1) else nb)
            if l == -1:
                got = [[jnp.where(exists, v, 0.0) for v in row] for row in got]
            one[l] = got if l in (0, 1) else [row + blank for row in got]
        for l in range(2):
            base = [
                [zero[l][f][b] + one[l][f][b] for b in range(nb)] for f in range(4)
            ]
            two = [[0.5 * v for v in row] for row in advance(one, base, l, nb)]
            slot = 2 + l if side == 0 else 1 - l
            for b in range(nb):
                for f in range(4):
                    turned[b, pl.ds(f * 32 + slot, 8, stride=4), :] = two[f][b]
                sums[b] = sums[b] + bent(two[0][b])
    for b in range(nb):
        zp[b * LANES : (b + 1) * LANES, :] = turned[b].T

    per = x_n // count_z
    scale = 8.0 / math.sqrt(h_n * LANES * count_z)
    for b in range(nb):
        path[b] = sums[b] * scale
    for b in range(nb):
        own[:, blk[b]] = path[b, pl.ds(gz * per, per), :]
        for k in range(1, count_z):
            sends[k - 1][:, blk[b]] = path[b, pl.ds((gz ^ k) * per, per), :]


def write_kernel(dims, pieces, s2, zp, *refs):
    x_n, h_n, ny = dims
    outs, (buf, sem) = refs[:4], refs[4:]
    lane = lane_iota()
    size = x_n // pieces
    copies = []
    for f in range(4):
        for x in range(x_n):
            for t in range(ny // 8):
                rows = slice(t * 8, t * 8 + 8)
                edge = pltpu.roll(zp[rows, :], (LANES - ((f * x_n + x) * 4 + 2)) % LANES, 1)
                for h in range(h_n):
                    cols = slice(h * LANES, (h + 1) * LANES)
                    v = s2[f, x, rows, cols]
                    if h == 0:
                        v = jnp.where(lane < 2, edge, v)
                    if h == h_n - 1:
                        v = jnp.where(lane >= LANES - 2, edge, v)
                    buf[f, x, rows, cols] = v
            if (x + 1) % size == 0:
                part = pl.ds(x + 1 - size, size)
                copies.append(
                    pltpu.make_async_copy(buf.at[f, part], outs[f].at[part], sem.at[f, x // size])
                )
                copies[-1].start()
    for c in copies:
        c.wait()


def pairs_of(count):
    a = [(i, i ^ 1) for i in range(count)]
    b = [(i, (i + 1) % count if i % 2 else (i - 1) % count) for i in range(count)]
    return a, b


def inner_pairs(count_z, count_y):
    pairs = []
    for z, other in pairs_of(count_z)[1]:
        for y in range(count_y):
            to = other * count_y + y if abs(z - other) == 1 else z * count_y + (y ^ 1)
            pairs.append((z * count_y + y, to))
    return pairs


def params(limit=LIMIT):
    return pltpu.CompilerParams(vmem_limit_bytes=limit)


def on_device(theta, u, v, w, markers):
    x_n, ny, nz = theta.shape
    h_n = nz // LANES
    count_z, count_y = lax.axis_size("gz"), lax.axis_size("gy")
    dims = (x_n, h_n, ny)
    nyp = ny + 2 * PAD
    f32 = jnp.float32
    fields = pltpu.VMEM((4, x_n, h_n, nyp, LANES), f32)
    args = [pltpu.with_memory_space_constraint(a, pltpu.HBM) for a in (theta, u, v, w, markers)]
    cells = x_n * ny * nz

    def cost(flops, moved):
        return pl.CostEstimate(flops=flops, bytes_accessed=moved, transcendentals=0)

    s0, mk, ys_a, ys_b, zown, zd = pl.pallas_call(
        functools.partial(pack_kernel, dims, 2),
        out_shape=(
            fields,
            pltpu.VMEM((x_n, h_n, nyp, LANES), jnp.int32),
            jax.ShapeDtypeStruct((72, nz), f32),
            jax.ShapeDtypeStruct((72, nz), f32),
            jax.ShapeDtypeStruct((2, 152, ny), f32),
            pltpu.VMEM((2, x_n, h_n, ny, LANES), f32),
        ),
        in_specs=[HBM] * 5,
        out_specs=(VMEM,) * 6,
        scratch_shapes=[
            pltpu.VMEM((3, ny, LANES), f32),
            pltpu.VMEM((3, ny // LANES, LANES, LANES), f32),
            pltpu.VMEM((2 * nz, 2 * nz), jnp.bfloat16),
            pltpu.SemaphoreType.DMA((2, 5, h_n)),
        ],
        compiler_params=params(),
        name="load_and_pack",
    )(*args)

    y_pairs = pairs_of(count_y)
    yb = lax.ppermute(ys_b, "gy", y_pairs[1])
    ya = lax.ppermute(ys_a, "gy", y_pairs[0])

    s1 = pl.pallas_call(
        functools.partial(section_one_kernel, dims),
        out_shape=fields,
        in_specs=[VMEM] * 3,
        out_specs=VMEM,
        compiler_params=params(),
        cost_estimate=cost(100 * cells, 36 * cells),
        name="section_one",
    )(s0, mk, zd)

    zs_a, zs_b = pl.pallas_call(
        functools.partial(corner_kernel, dims),
        out_shape=(jax.ShapeDtypeStruct((104, ny), f32),) * 2,
        in_specs=[VMEM] * 4,
        out_specs=(VMEM,) * 2,
        compiler_params=params(),
        name="corners",
    )(yb, ya, zown, s1)

    zb = lax.ppermute(zs_b, ("gz", "gy"), inner_pairs(count_z, count_y))
    za = lax.ppermute(zs_a, "gz", pairs_of(count_z)[0])

    s2, acc, _ = pl.pallas_call(
        functools.partial(section_two_kernel, dims),
        out_shape=(
            pltpu.VMEM((4, x_n, ny, nz), f32),
            pltpu.VMEM((x_n, ny, LANES), f32),
            fields,
        ),
        in_specs=[VMEM] * 5,
        out_specs=(VMEM,) * 3,
        input_output_aliases={2: 2},
        compiler_params=params(),
        cost_estimate=cost(110 * cells, 52 * cells),
        name="section_two",
    )(s0, mk, s1, yb, ya)

    per, nb = x_n // count_z, ny // LANES
    edges = pl.pallas_call(
        functools.partial(edge_kernel, dims, count_z),
        out_shape=(
            jax.ShapeDtypeStruct((ny, LANES), f32),
        )
        + (jax.ShapeDtypeStruct((per, ny), f32),) * count_z,
        in_specs=[VMEM] * 6,
        out_specs=(VMEM,) * (1 + count_z),
        scratch_shapes=[
            pltpu.VMEM((nb, LANES, LANES), f32),
            pltpu.VMEM((nb, x_n, LANES), f32),
        ],
        compiler_params=params(),
        name="edges",
    )(zown, yb, ya, zb, za, acc)
    zp, own = edges[:2]

    total = own
    for k in range(count_z - 1, 0, -1):
        total = total + lax.ppermute(
            edges[1 + k], "gz", [(i, i ^ k) for i in range(count_z)]
        )

    outs = pl.pallas_call(
        functools.partial(write_kernel, dims, 4),
        out_shape=(pltpu.HBM((x_n, ny, nz), f32),) * 4,
        in_specs=[VMEM] * 2,
        out_specs=(HBM,) * 4,
        scratch_shapes=[pltpu.VMEM((4, x_n, ny, nz), f32), pltpu.SemaphoreType.DMA((4, 4))],
        compiler_params=params(),
        cost_estimate=cost(cells, 32 * cells),
        name="write",
    )(s2, zp)
    return (*outs, total)


def solution(mesh):
    spec = P(None, "gy", "gz")
    return jax.shard_map(
        on_device,
        mesh=mesh,
        in_specs=(spec,) * 5,
        out_specs=(spec,) * 4 + (P("gz", "gy"),),
        check_vma=False,
    )
```

```python
import functools
import math

import jax
import jax.numpy as jnp
from jax import lax
from jax.experimental import pallas as pl
from jax.experimental.pallas import tpu as pltpu
from jax.sharding import PartitionSpec as P

TIME_STEP = 0.1
NU_BASE = 0.05
KAPPA_BASE = 0.05
SMAG_COEF = 0.03
PRANDTL = 0.4
BUOYANCY = 0.5
LANES = 128
PAD = 8
LIMIT = 16 << 20
HBM = pl.BlockSpec(memory_space=pltpu.HBM)
VMEM = pl.BlockSpec(memory_space=pltpu.VMEM)


def lane_iota():
    return lax.broadcasted_iota(jnp.int32, (8, LANES), 1)


def stepped(base, c, e, w, n, s, u, l, given=None):
    half = 0.5 * TIME_STEP
    given = given or {}
    dx = [a - b for a, b in zip(e, w)]
    dy = [a - b for a, b in zip(n, s)]
    dz = [given[f][0] if f in given else u[f] - l[f] for f in range(4)]
    lz = [given[f][1] if f in given else (u[f] + l[f]) - 6.0 * c[f] for f in range(4)]
    lap = [((a + b) + (p + q)) + t for a, b, p, q, t in zip(e, w, n, s, lz)]
    straight = dx[1] * dx[1] + dy[2] * dy[2] + dz[3] * dz[3]
    shear_a = dy[1] + dx[2]
    shear_b = dz[1] + dx[3]
    shear_c = dz[2] + dy[3]
    shear = shear_a * shear_a + shear_b * shear_b + shear_c * shear_c
    k = (2.0 * SMAG_COEF) ** 2
    arg = (straight + straight + shear) * (0.25 * k) + 0.01 * k
    eddy = arg * lax.rsqrt(arg)
    c_mom = eddy + 2.0 * NU_BASE
    c_heat = eddy * (1.0 / PRANDTL) + 2.0 * KAPPA_BASE
    out = []
    for f in range(4):
        rate = (c_heat if f == 0 else c_mom) * lap[f]
        rate = rate - (c[1] * dx[f] + c[2] * dy[f] + c[3] * dz[f])
        if f == 3:
            rate = rate + (c[0] if 2.0 * BUOYANCY == 1.0 else (2.0 * BUOYANCY) * c[0])
        out.append(base[f] + half * rate)
    return out


def bent(theta):
    return 1.0 - jnp.exp2(theta * (-0.125 * math.log2(math.e)))


def lane_next(blocks, lane):
    r = [pltpu.roll(b, LANES - 1, 1) for b in blocks]
    if len(r) == 1:
        return r
    return [jnp.where(lane == LANES - 1, r[(i + 1) % len(r)], r[i]) for i in range(len(r))]


def lane_prev(blocks, lane):
    r = [pltpu.roll(b, 1, 1) for b in blocks]
    if len(r) == 1:
        return r
    return [jnp.where(lane == 0, r[i - 1], r[i]) for i in range(len(r))]


def height_pair(blocks, lane):
    count = len(blocks)
    up = [pltpu.roll(b, LANES - 1, 1) for b in blocks]
    lo = [pltpu.roll(b, 1, 1) for b in blocks]
    upper = [
        up[i] if i == count - 1 else jnp.where(lane == LANES - 1, up[i + 1], up[i])
        for i in range(count)
    ]
    lower = [lo[i] if i == 0 else jnp.where(lane == 0, lo[i - 1], lo[i]) for i in range(count)]
    return upper, lower


def east(q):
    return pltpu.roll(q, 7, 0)


def west(q):
    return pltpu.roll(q, 1, 0)


def flat(ref):
    return ref.reshape(math.prod(ref.shape[:-1]), LANES)


def row_of(ref, lead, x_stride, start, x):
    return ref[pl.ds(lead + start, x, stride=x_stride), :]


def height_matrix(nz):
    i = lax.broadcasted_iota(jnp.int32, (nz, 2 * nz), 0)
    j = lax.broadcasted_iota(jnp.int32, (nz, 2 * nz), 1)
    d = jnp.where(j < nz, i - j, i - j + nz)
    one, next_one = jnp.where(d == 1, 1.0, 0.0), jnp.where(d == -1, 1.0, 0.0)
    out = jnp.where(j < nz, one - next_one, one + next_one - jnp.where(d == 0, 6.0, 0.0))
    return out.astype(jnp.bfloat16)


def height_differences(rows, matrix):
    high = rows.astype(jnp.bfloat16)
    rest = (rows - high.astype(jnp.float32)).astype(jnp.bfloat16)
    return jnp.dot(
        jnp.concatenate([high, rest], axis=1), matrix, preferred_element_type=jnp.float32
    )


def pack_kernel(dims, parts, *refs):
    x_n, h_n, ny = dims
    ins = refs[:5]
    s0, mk, ys_a, ys_b, zown, zd, part, turned, matrix, sem = refs[5:]
    nyp = ny + 2 * PAD
    lane = lane_iota()
    sub = lax.broadcasted_iota(jnp.int32, (8, LANES), 0)
    size = ny // parts
    copies = []
    for p in range(parts):
        for f in range(5):
            for h in range(h_n):
                dst = s0.at[f] if f < 4 else mk
                copies.append(
                    pltpu.make_async_copy(
                        ins[f].at[:, pl.ds(p * size, size), pl.ds(h * LANES, LANES)],
                        dst.at[:, h, pl.ds(PAD + p * size, size), :],
                        sem.at[p, f, h],
                    )
                )
    for c in copies:
        c.start()
    group = lane // 8

    nz = h_n * LANES
    once = height_matrix(nz)
    matrix[0:nz, :] = once
    matrix[nz:, :] = once

    def heights(p):
        rows = slice(PAD + p * size, PAD + (p + 1) * size)
        q = jnp.concatenate(
            [
                jnp.concatenate([s0[0, x, h, rows, :] for h in range(h_n)], axis=1)
                for x in range(x_n)
            ],
            axis=0,
        )
        got = height_differences(q, matrix[...])
        for x in range(x_n):
            for h in range(h_n):
                for n in range(2):
                    at = n * nz + h * LANES
                    zd[n, x, h, p * size : (p + 1) * size, :] = got[
                        x * size : (x + 1) * size, at : at + LANES
                    ]

    def columns(t):
        y = PAD + t * 8
        for a in range(2):
            acc = jnp.zeros((8, LANES), jnp.float32)
            for g in range(16):
                f, x = a * 2 + g // 8, g % 8
                lo, hi = s0[f, x, 0, pl.ds(y, 8), :], s0[f, x, h_n - 1, pl.ds(y, 8), :]
                both = jnp.where(lane < LANES // 2, lo, hi)
                acc = jnp.where(group == g, pltpu.roll(both, (g * 8 + 4) % LANES, 1), acc)
            part[a, pl.ds(t * 8, 8), :] = acc
        bits = jnp.zeros((8, LANES), jnp.int32)
        for x in range(x_n):
            lo, hi = mk[x, 0, pl.ds(y, 8), :], mk[x, h_n - 1, pl.ds(y, 8), :]
            bits = bits + jnp.where(lane < LANES // 2, lo, hi) * (1 << x)
        part[2, pl.ds(t * 8, 8), :] = bits.astype(jnp.float32)

    for p in range(parts):
        for c in copies[p * 5 * h_n : (p + 1) * 5 * h_n]:
            c.wait()
        for t in range(p * size // 8, (p + 1) * size // 8):
            columns(t)
        heights(p)

    even = lax.rem(lax.axis_index("gy"), 2) == 0
    s0_flat, mk_flat = flat(s0), flat(mk)
    stride = h_n * nyp
    for h in range(h_n):
        cols = slice(h * LANES, (h + 1) * LANES)
        for k in range(9):
            r, f = k // 4 % 2, k % 4

            def row(y):
                if k == 8:
                    return row_of(mk_flat, h * nyp, stride, PAD + y, x_n).astype(jnp.float32)
                return row_of(s0_flat, (f * x_n * h_n + h) * nyp, stride, PAD + y, x_n)

            first, last = row(r), row(ny - 1 - r)
            ys_a[k * 8 : k * 8 + 8, cols] = jnp.where(even, last, first)
            ys_b[k * 8 : k * 8 + 8, cols] = jnp.where(even, first, last)

    bit = jnp.zeros((8, LANES), jnp.int32)
    for x in range(x_n):
        bit = jnp.where(sub == x, 1 << x, bit)
    for b in range(ny // LANES):
        cols = slice(b * LANES, (b + 1) * LANES)
        for a in range(3):
            turned[a, b] = part[a, cols, :].T
        for side in range(2):
            for l in range(4):
                j = 4 + l if side == 0 else 3 - l
                for f in range(4):
                    k = f * 4 + l
                    zown[side, k * 8 : k * 8 + 8, cols] = turned[
                        f // 2, b, pl.ds((f % 2) * 64 + j, 8, stride=8), :
                    ]
                if l < 3:
                    k, at = 16 + l, l if side == 0 else LANES - 1 - l
                    row = jnp.broadcast_to(turned[2, b, at : at + 1, :], (8, LANES))
                    has = jnp.bitwise_and(row.astype(jnp.int32), bit) != 0
                    zown[side, k * 8 : k * 8 + 8, cols] = jnp.where(has, 1.0, 0.0)


def y_halo(even, a_ref, b_ref, k, cols):
    a, b = a_ref[k * 8 : k * 8 + 8, cols], b_ref[k * 8 : k * 8 + 8, cols]
    return jnp.where(even, b, a), jnp.where(even, a, b)


def beyond(lane, even, ya, yb, h_n, side, f, l, rows):
    h = 0 if side == 0 else h_n - 1
    at = l if side == 0 else LANES - 1 - l
    out = jnp.zeros((8, LANES), jnp.float32)
    for r in rows:
        k = r * 4 + f if f < 4 else 8
        before, after = y_halo(even, ya, yb, k, slice(h * LANES, (h + 1) * LANES))
        out = jnp.where(
            lane == LANES - 1 - r, pltpu.roll(before, (LANES - 1 - r - at) % LANES, 1), out
        )
        out = jnp.where(lane == r, pltpu.roll(after, (r - at) % LANES, 1), out)
    return out


def corner_kernel(dims, yb, ya, zown, after, zs_a, zs_b):
    del after
    x_n, h_n, ny = dims
    lane = lane_iota()
    even = lax.rem(lax.axis_index("gy"), 2) == 0
    even_z = lax.rem(lax.axis_index("gz"), 2) == 0

    def strip(dst, side):
        for l in range(2):
            for f in range(4):
                k, m = l * 4 + f, f * 4 + l
                dst[k * 8 : k * 8 + 8, :] = zown[side, m * 8 : m * 8 + 8, :]
        dst[64:72, :] = zown[side, 128:136, :]
        for f in range(4):
            dst[72 + f * 8 : 80 + f * 8, 0:LANES] = beyond(
                lane, even, ya, yb, h_n, side, f, 0, (0,)
            )
            if ny > LANES:
                dst[72 + f * 8 : 80 + f * 8, LANES:] = jnp.zeros((8, ny - LANES), jnp.float32)

    @pl.when(even_z)
    def _():
        strip(zs_a, 1)
        strip(zs_b, 0)

    @pl.when(jnp.logical_not(even_z))
    def _():
        strip(zs_a, 0)
        strip(zs_b, 1)


def load4(ref, x, h, y):
    return [ref[f, x, h, pl.ds(y, 8), :] for f in range(4)]


def section_one_kernel(dims, s0, mk, zd, s1):
    x_n, h_n, ny = dims
    lane = lane_iota()

    def tile(y, yo, x):
        c = [load4(s0, x, h, y) for h in range(h_n)]
        pairs = [None] + [height_pair([c[h][f] for h in range(h_n)], lane) for f in range(1, 4)]
        for h in range(h_n):
            r = stepped(
                c[h],
                c[h],
                load4(s0, (x + 1) % x_n, h, y),
                load4(s0, (x - 1) % x_n, h, y),
                load4(s0, x, h, y + 1),
                load4(s0, x, h, y - 1),
                [None] + [p[0][h] for p in pairs[1:]],
                [None] + [p[1][h] for p in pairs[1:]],
                {0: [zd[n, x, h, pl.ds(yo, 8), :] for n in range(2)]},
            )
            open_cell = mk[x, h, pl.ds(y, 8), :] != 0
            s1[0, x, h, pl.ds(y, 8), :] = r[0]
            for f in range(1, 4):
                s1[f, x, h, pl.ds(y, 8), :] = jnp.where(open_cell, r[f], 0.0)

    for t in range(ny // 8):
        for x in range(x_n):
            tile(PAD + t * 8, t * 8, x)


def outer_rows(dims, s0, mk, ya, yb, s1):
    x_n, h_n, ny = dims
    nyp = ny + 2 * PAD
    lane = lane_iota()
    even = lax.rem(lax.axis_index("gy"), 2) == 0
    s0_flat, s1_flat, mk_flat = flat(s0), flat(s1), flat(mk)
    stride = h_n * nyp
    blk = [slice(h * LANES, (h + 1) * LANES) for h in range(h_n)]
    for side in range(2):

        def start(f, h, r):
            return (f * x_n * h_n + h) * nyp + PAD + (r if side == 0 else ny - 1 - r)

        def halo(k):
            return [y_halo(even, ya, yb, k, blk[h])[side] for h in range(h_n)]

        zero = {-2: [halo(4 + f) for f in range(4)], -1: [halo(f) for f in range(4)]}
        for r in range(2):
            zero[r] = [
                [row_of(s0_flat, 0, stride, start(f, h, r), x_n) for h in range(h_n)]
                for f in range(4)
            ]
        open_at = {
            -1: [m != 0.0 for m in halo(8)],
            0: [row_of(mk_flat, 0, stride, start(0, h, 0), x_n) != 0 for h in range(h_n)],
        }
        for r in (-1, 0):
            pairs = [height_pair(zero[r][f], lane) for f in range(4)]
            ahead, behind = (r + 1, r - 1) if side == 0 else (r - 1, r + 1)
            for h in range(h_n):
                c = [zero[r][f][h] for f in range(4)]
                q = stepped(
                    c,
                    c,
                    [east(v) for v in c],
                    [west(v) for v in c],
                    [zero[ahead][f][h] for f in range(4)],
                    [zero[behind][f][h] for f in range(4)],
                    [p[0][h] for p in pairs],
                    [p[1][h] for p in pairs],
                )
                for f in range(4):
                    v = q[f] if f == 0 else jnp.where(open_at[r][h], q[f], 0.0)
                    s1_flat[pl.ds(start(f, h, r), x_n, stride=stride), :] = v


def section_two_kernel(dims, s0, mk, s1_in, yb, ya, s2, acc, s1):
    del s1_in
    x_n, h_n, ny = dims
    lane = lane_iota()

    def tile(y, yo, x):
        c = [load4(s1, x, h, y) for h in range(h_n)]
        pairs = [height_pair([c[h][f] for h in range(h_n)], lane) for f in range(4)]
        total = None
        for h in range(h_n):
            start = load4(s0, x, h, y)
            r = stepped(
                [a + b for a, b in zip(start, c[h])],
                c[h],
                load4(s1, (x + 1) % x_n, h, y),
                load4(s1, (x - 1) % x_n, h, y),
                load4(s1, x, h, y + 1),
                load4(s1, x, h, y - 1),
                [p[0][h] for p in pairs],
                [p[1][h] for p in pairs],
            )
            part = jnp.where(mk[x, h, pl.ds(y, 8), :] != 0, 0.5, 0.0)
            theta = 0.5 * r[0]
            cols = slice(h * LANES, (h + 1) * LANES)
            s2[0, x, pl.ds(yo, 8), cols] = theta
            for f in range(1, 4):
                s2[f, x, pl.ds(yo, 8), cols] = part * r[f]
            refr = bent(theta)
            if h == 0:
                refr = jnp.where(lane < 2, 0.0, refr)
            if h == h_n - 1:
                refr = jnp.where(lane >= LANES - 2, 0.0, refr)
            total = refr if total is None else total + refr
        return total

    def tiles(places):
        for t in places:
            for x in range(x_n):
                acc[x, t * 8 : t * 8 + 8, :] = tile(PAD + t * 8, t * 8, x)

    last = ny // 8 - 1
    tiles(range(1, last))
    outer_rows(dims, s0, mk, ya, yb, s1)
    tiles((0, last))


def lane_sums(acc, b):
    x_n = acc.shape[0]
    rows = acc[:, b * LANES : (b + 1) * LANES, :].reshape(x_n * LANES, LANES)
    ones = jnp.ones((LANES, LANES), jnp.bfloat16)
    total = None
    for _ in range(3):
        piece = rows.astype(jnp.bfloat16)
        rows = rows - piece.astype(jnp.float32)
        got = jnp.dot(piece, ones, preferred_element_type=jnp.float32)
        total = got if total is None else total + got
    shape = (LANES, LANES)
    diagonal = lax.broadcasted_iota(jnp.int32, shape, 0) == lax.broadcasted_iota(
        jnp.int32, shape, 1
    )
    sub = lax.broadcasted_iota(jnp.int32, (8, LANES), 0)
    out = jnp.zeros((8, LANES), jnp.float32)
    for x in range(x_n):
        part = jnp.where(diagonal, total[x * LANES : (x + 1) * LANES], 0.0)
        out = jnp.where(sub == x, jnp.sum(part, axis=0, keepdims=True), out)
    return out


def edge_kernel(dims, count_z, *refs):
    x_n, h_n, ny = dims
    zown, yb, ya, za, zb, acc = refs[:6]
    zp, own = refs[6:8]
    sends = refs[8 : 8 + count_z - 1]
    turned, path = refs[8 + count_z - 1 :]
    nb = ny // LANES
    lane = lane_iota()
    even = lax.rem(lax.axis_index("gy"), 2) == 0
    gz = lax.axis_index("gz")
    even_z = lax.rem(gz, 2) == 0
    blk = [slice(b * LANES, (b + 1) * LANES) for b in range(nb)]

    sums = [lane_sums(acc, b) for b in range(nb)]

    for side in range(2):
        exists = (gz > 0) if side == 0 else (gz < count_z - 1)

        def halo(k):
            cols = [slice(b * LANES, (b + 1) * LANES) for b in range(nb)]
            rows = slice(k * 8, k * 8 + 8)
            take_a = jnp.logical_not(even_z) if side == 0 else even_z
            got = [jnp.where(take_a, za[rows, c], zb[rows, c]) for c in cols]
            return [jnp.where(exists, v, 0.0) for v in got]

        def mine(k):
            return [zown[side, k * 8 : k * 8 + 8, blk[b]] for b in range(nb)]

        def extra(f, l, rows):
            return [beyond(lane, even, ya, yb, h_n, side, f, l, rows)]

        blank = [jnp.zeros((8, LANES), jnp.float32)]
        zero = {
            -2: [halo(4 + f) + blank for f in range(4)],
            -1: [halo(f) + halo(9 + f)[:1] for f in range(4)],
        }
        for l in range(4):
            zero[l] = [
                mine(f * 4 + l) + (extra(f, l, (0, 1)) if l < 3 else blank) for f in range(4)
            ]
        open_at = {-1: [m != 0.0 for m in halo(8)]}
        for l in range(3):
            open_at[l] = [m != 0.0 for m in mine(16 + l)]
        for l in range(2):
            open_at[l] = open_at[l] + [extra(4, l, (0,))[0] != 0.0]

        def advance(state, base, l, blocks):
            norths = [lane_next(state[l][f], lane) for f in range(4)]
            souths = [lane_prev(state[l][f], lane) for f in range(4)]
            above, below = (l + 1, l - 1) if side == 0 else (l - 1, l + 1)
            out = [[None] * blocks for _ in range(4)]
            for b in range(blocks):
                c = [state[l][f][b] for f in range(4)]
                q = stepped(
                    [base[f][b] for f in range(4)],
                    c,
                    [east(v) for v in c],
                    [west(v) for v in c],
                    [norths[f][b] for f in range(4)],
                    [souths[f][b] for f in range(4)],
                    [state[above][f][b] for f in range(4)],
                    [state[below][f][b] for f in range(4)],
                )
                for f in range(4):
                    out[f][b] = q[f] if f == 0 else jnp.where(open_at[l][b], q[f], 0.0)
            return out

        one = {}
        for l in range(-1, 3):
            got = advance(zero, zero[l], l, nb + 1 if l in (0, 1) else nb)
            if l == -1:
                got = [[jnp.where(exists, v, 0.0) for v in row] for row in got]
            one[l] = got if l in (0, 1) else [row + blank for row in got]
        for l in range(2):
            base = [
                [zero[l][f][b] + one[l][f][b] for b in range(nb)] for f in range(4)
            ]
            two = [[0.5 * v for v in row] for row in advance(one, base, l, nb)]
            slot = 2 + l if side == 0 else 1 - l
            for b in range(nb):
                for f in range(4):
                    turned[b, pl.ds(f * 32 + slot, 8, stride=4), :] = two[f][b]
                sums[b] = sums[b] + bent(two[0][b])
    for b in range(nb):
        zp[b * LANES : (b + 1) * LANES, :] = turned[b].T

    per = x_n // count_z
    scale = 8.0 / math.sqrt(h_n * LANES * count_z)
    for b in range(nb):
        path[b] = sums[b] * scale
    for b in range(nb):
        own[:, blk[b]] = path[b, pl.ds(gz * per, per), :]
        for k in range(1, count_z):
            sends[k - 1][:, blk[b]] = path[b, pl.ds((gz ^ k) * per, per), :]


def write_kernel(dims, pieces, s2, zp, *refs):
    x_n, h_n, ny = dims
    outs, (buf, sem) = refs[:4], refs[4:]
    lane = lane_iota()
    size = x_n // pieces
    copies = []
    for f in range(4):
        for x in range(x_n):
            for t in range(ny // 8):
                rows = slice(t * 8, t * 8 + 8)
                edge = pltpu.roll(zp[rows, :], (LANES - ((f * x_n + x) * 4 + 2)) % LANES, 1)
                for h in range(h_n):
                    cols = slice(h * LANES, (h + 1) * LANES)
                    v = s2[f, x, rows, cols]
                    if h == 0:
                        v = jnp.where(lane < 2, edge, v)
                    if h == h_n - 1:
                        v = jnp.where(lane >= LANES - 2, edge, v)
                    buf[f, x, rows, cols] = v
            if (x + 1) % size == 0:
                part = pl.ds(x + 1 - size, size)
                copies.append(
                    pltpu.make_async_copy(buf.at[f, part], outs[f].at[part], sem.at[f, x // size])
                )
                copies[-1].start()
    for c in copies:
        c.wait()


def pairs_of(count):
    a = [(i, i ^ 1) for i in range(count)]
    b = [(i, (i + 1) % count if i % 2 else (i - 1) % count) for i in range(count)]
    return a, b


def inner_pairs(count_z, count_y):
    pairs = []
    for z, other in pairs_of(count_z)[1]:
        for y in range(count_y):
            to = other * count_y + y if abs(z - other) == 1 else z * count_y + (y ^ 1)
            pairs.append((z * count_y + y, to))
    return pairs


def params(limit=LIMIT):
    return pltpu.CompilerParams(vmem_limit_bytes=limit)


def on_device(theta, u, v, w, markers):
    x_n, ny, nz = theta.shape
    h_n = nz // LANES
    count_z, count_y = lax.axis_size("gz"), lax.axis_size("gy")
    dims = (x_n, h_n, ny)
    nyp = ny + 2 * PAD
    f32 = jnp.float32
    fields = pltpu.VMEM((4, x_n, h_n, nyp, LANES), f32)
    args = [pltpu.with_memory_space_constraint(a, pltpu.HBM) for a in (theta, u, v, w, markers)]
    cells = x_n * ny * nz

    def cost(flops, moved):
        return pl.CostEstimate(flops=flops, bytes_accessed=moved, transcendentals=0)

    s0, mk, ys_a, ys_b, zown, zd = pl.pallas_call(
        functools.partial(pack_kernel, dims, 2),
        out_shape=(
            fields,
            pltpu.VMEM((x_n, h_n, nyp, LANES), jnp.int32),
            jax.ShapeDtypeStruct((72, nz), f32),
            jax.ShapeDtypeStruct((72, nz), f32),
            jax.ShapeDtypeStruct((2, 152, ny), f32),
            pltpu.VMEM((2, x_n, h_n, ny, LANES), f32),
        ),
        in_specs=[HBM] * 5,
        out_specs=(VMEM,) * 6,
        scratch_shapes=[
            pltpu.VMEM((3, ny, LANES), f32),
            pltpu.VMEM((3, ny // LANES, LANES, LANES), f32),
            pltpu.VMEM((2 * nz, 2 * nz), jnp.bfloat16),
            pltpu.SemaphoreType.DMA((2, 5, h_n)),
        ],
        compiler_params=params(),
        name="load_and_pack",
    )(*args)

    y_pairs = pairs_of(count_y)
    yb = lax.ppermute(ys_b, "gy", y_pairs[1])
    ya = lax.ppermute(ys_a, "gy", y_pairs[0])

    s1 = pl.pallas_call(
        functools.partial(section_one_kernel, dims),
        out_shape=fields,
        in_specs=[VMEM] * 3,
        out_specs=VMEM,
        compiler_params=params(),
        cost_estimate=cost(100 * cells, 36 * cells),
        name="section_one",
    )(s0, mk, zd)

    zs_a, zs_b = pl.pallas_call(
        functools.partial(corner_kernel, dims),
        out_shape=(jax.ShapeDtypeStruct((104, ny), f32),) * 2,
        in_specs=[VMEM] * 4,
        out_specs=(VMEM,) * 2,
        compiler_params=params(),
        name="corners",
    )(yb, ya, zown, s1)

    zb = lax.ppermute(zs_b, ("gz", "gy"), inner_pairs(count_z, count_y))
    za = lax.ppermute(zs_a, "gz", pairs_of(count_z)[0])

    s2, acc, _ = pl.pallas_call(
        functools.partial(section_two_kernel, dims),
        out_shape=(
            pltpu.VMEM((4, x_n, ny, nz), f32),
            pltpu.VMEM((x_n, ny, LANES), f32),
            fields,
        ),
        in_specs=[VMEM] * 5,
        out_specs=(VMEM,) * 3,
        input_output_aliases={2: 2},
        compiler_params=params(),
        cost_estimate=cost(110 * cells, 52 * cells),
        name="section_two",
    )(s0, mk, s1, yb, ya)

    per, nb = x_n // count_z, ny // LANES
    edges = pl.pallas_call(
        functools.partial(edge_kernel, dims, count_z),
        out_shape=(
            jax.ShapeDtypeStruct((ny, LANES), f32),
        )
        + (jax.ShapeDtypeStruct((per, ny), f32),) * count_z,
        in_specs=[VMEM] * 6,
        out_specs=(VMEM,) * (1 + count_z),
        scratch_shapes=[
            pltpu.VMEM((nb, LANES, LANES), f32),
            pltpu.VMEM((nb, x_n, LANES), f32),
        ],
        compiler_params=params(),
        name="edges",
    )(zown, yb, ya, za, zb, acc)
    zp, own = edges[:2]

    total = own
    for k in (3, 1, 2) if count_z == 4 else range(count_z - 1, 0, -1):
        total = total + lax.ppermute(
            edges[1 + k], "gz", [(i, i ^ k) for i in range(count_z)]
        )

    outs = pl.pallas_call(
        functools.partial(write_kernel, dims, 4),
        out_shape=(pltpu.HBM((x_n, ny, nz), f32),) * 4,
        in_specs=[VMEM] * 2,
        out_specs=(HBM,) * 4,
        scratch_shapes=[pltpu.VMEM((4, x_n, ny, nz), f32), pltpu.SemaphoreType.DMA((4, 4))],
        compiler_params=params(),
        cost_estimate=cost(cells, 32 * cells),
        name="write",
    )(s2, zp)
    return (*outs, total)


def solution(mesh):
    spec = P(None, "gy", "gz")
    return jax.shard_map(
        on_device,
        mesh=mesh,
        in_specs=(spec,) * 5,
        out_specs=(spec,) * 4 + (P("gz", "gy"),),
        check_vma=False,
    )
```
